128 devices in a mesh: ctx: 16 (over z_lo, x, core), col: 8 (over z_hi, y).
Axes of the slice: x: 4, y: 4, z: 4 (z_hi: 2, z_lo: 2; z = z_hi * 2 + z_lo), core: 2. Of those that a mesh axis runs over, the one named last changes fastest.
Arguments:
- sequence: bfloat16 [16384, 1536], P('ctx'), may hold values from -32 to 32
- norm_gain: bfloat16 [1536], replicated, may hold values from 0.099609375 to 1.8984375
- query_weight: bfloat16 [1536, 1536], P(None, 'col')
- key_weight: bfloat16 [1536, 1536], P(None, 'col')
- value_weight: bfloat16 [1536, 1536], P(None, 'col')
- out_weight: bfloat16 [1536, 1536], replicated, may hold values from -0.15625 to 0.15625
- pool_gain: bfloat16 [1536], replicated, may hold values from 0.099609375 to 1.8984375
- row_weight: bfloat16 [1536, 128], replicated, may hold values from -0.15625 to 0.15625
- column_weight: bfloat16 [1536, 128], replicated, may hold values from -0.15625 to 0.15625
- conv_near: bfloat16 [3, 3, 128, 128], replicated, may hold values from -0.1875 to 0.1875
- conv_far: bfloat16 [3, 3, 128, 128], replicated, may hold values from -0.1875 to 0.1875
- trans_gain: bfloat16 [128], replicated, may hold values from 0.099609375 to 1.8984375
- trans_in: bfloat16 [128, 512], replicated, may hold values from -0.5 to 0.5
- trans_out: bfloat16 [512, 128], replicated, may hold values from -0.25 to 0.25
Outputs:
- trunk_out: bfloat16 [16384, 1536], P('ctx', 'col')
- pair_out: bfloat16 [1024, 1024, 128], P('ctx', 'col')
The draws below stay inside these ranges and needn't reach their ends.
All inputs are finite; a program needn't handle non-finite values.
Results may differ from the reference program's by a relative error of at most 0.025.
The reference program's roundings to bfloat16 on the way (of `normed`, `attended`, `scaled`, `near`, `far`, `layer` and `middle`) count: a program that leaves them out, or rounds other values in their place, can miss the bound.
Values may be sent and summed in bfloat16 or wider, within the bound.
No kernel may reach another device: no remote copies, remote signals or barrier semaphores. Data moves between devices by JAX's collectives and lax.ppermute only.
A program may use at most 192 MiB of HBM per device.

```python
import math
import jax
import jax.numpy as jnp
from jax import lax

D = 1536
HEADS = 8
C = 128
TRANS = 512
POOL = 16
HEAD = 192
SEQ = 16384
PAIR = 1024


def scaled_weight(key, factor):
    normal_part = jnp.clip(jax.random.normal(key, (D, D), jnp.float32), -4.0, 4.0)
    return normal_part * factor


def draw_sequence(key, part):
    key = jax.random.fold_in(key, 1)
    first_key = jax.random.fold_in(key, 0)
    return jnp.clip(jax.random.normal(first_key, (SEQ, D), jnp.float32), -6.0, 6.0).astype(jnp.bfloat16)


def draw_query_weight(key, part):
    key = jax.random.fold_in(key, 2)
    return scaled_weight(key, 2.5 / math.sqrt(D)).astype(jnp.bfloat16)


def draw_key_weight(key, part):
    key = jax.random.fold_in(key, 3)
    return scaled_weight(key, 1.0 / math.sqrt(D)).astype(jnp.bfloat16)


def draw_value_weight(key, part):
    key = jax.random.fold_in(key, 4)
    return scaled_weight(key, 1.0 / math.sqrt(D)).astype(jnp.bfloat16)


def noise(stream_key, shape, width, limit, kind=jnp.bfloat16):
    return jnp.clip(width * jax.random.normal(stream_key, shape, jnp.float32), -limit, limit).astype(kind)


def setup_inputs(seed: int = 0) -> dict:
    streams_of = jax.random.split(jax.random.key(seed), 15)
    return {
        "sequence": draw_sequence(jax.random.fold_in(streams_of[14], 71), 0),
        "norm_gain": jnp.clip(1.0 + 0.18 * jax.random.normal(streams_of[1], (D,), jnp.float32), 0.099609375, 1.8984375).astype(jnp.bfloat16),
        "query_weight": draw_query_weight(jax.random.fold_in(streams_of[14], 71), 0),
        "key_weight": draw_key_weight(jax.random.fold_in(streams_of[14], 71), 0),
        "value_weight": draw_value_weight(jax.random.fold_in(streams_of[14], 71), 0),
        "out_weight": noise(streams_of[5], (D, D), D ** -0.5, 0.15625),
        "pool_gain": jnp.clip(1.0 + 0.18 * jax.random.normal(streams_of[6], (D,), jnp.float32), 0.099609375, 1.8984375).astype(jnp.bfloat16),
        "row_weight": noise(streams_of[7], (D, C), D ** -0.5, 0.15625),
        "column_weight": noise(streams_of[8], (D, C), D ** -0.5, 0.15625),
        "conv_near": noise(streams_of[9], (3, 3, C, C), (9 * C) ** -0.5, 0.1875),
        "conv_far": noise(streams_of[10], (3, 3, C, C), (9 * C) ** -0.5, 0.1875),
        "trans_gain": jnp.clip(1.0 + 0.18 * jax.random.normal(streams_of[11], (C,), jnp.float32), 0.099609375, 1.8984375).astype(jnp.bfloat16),
        "trans_in": noise(streams_of[12], (C, TRANS), C ** -0.5, 0.5),
        "trans_out": noise(streams_of[13], (TRANS, C), TRANS ** -0.5, 0.25),
    }


EPSILON = 1e-06
LAYER_EPSILON = 1e-05

def rms_rows(values, gain_vector):
    square_mean = lax.optimization_barrier(jnp.mean(values * values, axis=-1, keepdims=True))
    return values * lax.rsqrt(square_mean + EPSILON) * gain_vector.astype(jnp.float32)

def dilated_conv(hidden, kernel, dilation):
    result = lax.conv_general_dilated(hidden.astype(jnp.float32)[None], kernel.astype(jnp.float32), (1, 1), ((dilation, dilation), (dilation, dilation)), rhs_dilation=(dilation, dilation), dimension_numbers=('NHWC', 'HWIO', 'NHWC'), precision=lax.Precision.HIGHEST)
    return result[0]

def attend(queries, keys_head, values_head):
    factor = HEAD ** (-0.5)

    def block_rows(query_block):
        scores = jnp.dot(query_block, keys_head.T, preferred_element_type=jnp.float32) * factor
        weights = jnp.exp(scores - lax.optimization_barrier(jnp.max(scores, axis=-1, keepdims=True)))
        totals = lax.optimization_barrier(jnp.sum(weights, axis=-1, keepdims=True))
        mixed = jnp.dot(weights.astype(jnp.bfloat16), values_head, preferred_element_type=jnp.float32) / totals
        return mixed.astype(jnp.bfloat16)
    blocks = lax.map(block_rows, queries.reshape(SEQ // 512, 512, HEAD))
    return blocks.reshape(SEQ, HEAD)

def split_heads(matrix):
    return matrix.reshape(SEQ, HEADS, HEAD).transpose(1, 0, 2)

def one_head(triple):
    return attend(triple[0], triple[1], triple[2])

def reference(sequence, norm_gain, query_weight, key_weight, value_weight, out_weight, pool_gain, row_weight, column_weight, conv_near, conv_far, trans_gain, trans_in, trans_out):
    inputs = sequence.astype(jnp.float32)
    normed = rms_rows(inputs, norm_gain).astype(jnp.bfloat16)
    queries = jnp.dot(normed, query_weight, preferred_element_type=jnp.float32).astype(jnp.bfloat16)
    keys_all = jnp.dot(normed, key_weight, preferred_element_type=jnp.float32).astype(jnp.bfloat16)
    values_all = jnp.dot(normed, value_weight, preferred_element_type=jnp.float32).astype(jnp.bfloat16)
    attended = lax.map(one_head, (split_heads(queries), split_heads(keys_all), split_heads(values_all)))
    attended = attended.transpose(1, 0, 2).reshape(SEQ, D)
    trunk = inputs + jnp.dot(attended, out_weight, preferred_element_type=jnp.float32)
    trunk_out = trunk.astype(jnp.bfloat16)
    pooled = trunk_out.astype(jnp.float32).reshape(PAIR, POOL, D).mean(axis=1)
    inverse = lax.rsqrt(lax.optimization_barrier(jnp.mean(pooled * pooled, axis=-1, keepdims=True)) + EPSILON)
    scaled = (pooled * pool_gain.astype(jnp.float32)).astype(jnp.bfloat16)
    row_features = (inverse * jnp.dot(scaled, row_weight, preferred_element_type=jnp.float32)).astype(jnp.bfloat16)
    column_features = (inverse * jnp.dot(scaled, column_weight, preferred_element_type=jnp.float32)).astype(jnp.bfloat16)
    base = row_features.astype(jnp.float32)[:, None, :] + column_features.astype(jnp.float32)[None, :, :]
    near = jnp.maximum(base, 0.0).astype(jnp.bfloat16)
    first = base + dilated_conv(near, conv_near, 2)
    far = jnp.maximum(first, 0.0).astype(jnp.bfloat16)
    second = first + dilated_conv(far, conv_far, 4)
    centred = second - lax.optimization_barrier(jnp.mean(second, axis=-1, keepdims=True))
    variance = lax.optimization_barrier(jnp.mean(centred * centred, axis=-1, keepdims=True))
    layer = (centred * lax.rsqrt(variance + LAYER_EPSILON) * trans_gain.astype(jnp.float32)).astype(jnp.bfloat16)
    middle = jnp.maximum(jnp.dot(layer.reshape(PAIR * PAIR, C), trans_in, preferred_element_type=jnp.float32), 0.0).astype(jnp.bfloat16)
    update = jnp.dot(middle, trans_out, preferred_element_type=jnp.float32).reshape(PAIR, PAIR, C)
    pair_out = (second + update).astype(jnp.bfloat16)
    return (trunk_out, pair_out)
```

```python
import functools
import math

import jax
import jax.numpy as jnp
from jax import lax
from jax.experimental import pallas as pl
from jax.experimental.pallas import tpu as pltpu
from jax.sharding import PartitionSpec as P

POOL = 16
HEAD = 192
EPSILON = 1e-06
LAYER_EPSILON = 1e-05
OUTSIDE = -1e30
SCALE = math.log2(math.e) / math.sqrt(HEAD)
bf16 = jnp.bfloat16
f32 = jnp.float32
VMEM = 56 * 2**20


def params(limit=VMEM):
    return pltpu.CompilerParams(vmem_limit_bytes=limit)


def lanes_of(shape):
    return lax.broadcasted_iota(jnp.int32, shape, len(shape) - 1)


def pack_lanes(low, high):
    rolled = pltpu.roll(high, 64, axis=1)
    middle = jnp.where(lanes_of(rolled.shape) < 64, pltpu.roll(low, 128, axis=1), rolled)
    return jnp.concatenate([low[:, :128], middle], axis=1)


def unpack_query(packed):
    wide = pltpu.roll(packed[:, :256].astype(f32), 64, axis=1)
    lane = lanes_of(wide.shape)
    low = jnp.where(lane < 64, 0.0, wide).astype(bf16)
    high = jnp.where(lane < 64, 0.0, packed[:, 128:].astype(f32)).astype(bf16)
    return jnp.concatenate([low, high], axis=0)


def project_kernel(low_ref, high_ref, gain_ref, wq_ref, wk_ref, wv_ref, kv_ref, q_ref, ml_ref, mh_ref):
    gain = gain_ref[...].astype(f32)
    rows = low_ref.shape[0]
    part = rows // 2

    def wide(normed, w_ref):
        y = lax.dot_general(normed, w_ref[...], (((1,), (1,)), ((), ())), preferred_element_type=f32)
        return jnp.concatenate([y, jnp.zeros((y.shape[0], 64), f32)], axis=1)

    for start in range(0, rows, part):
        halves = []
        for ref, mean_ref in ((low_ref, ml_ref), (high_ref, mh_ref)):
            x = ref[start : start + part, :].astype(f32)
            mean = jnp.mean(x.reshape(part // POOL, POOL, x.shape[1]), axis=1)
            mean_ref[start // POOL : (start + part) // POOL, :] = mean
            square = jnp.mean(x * x, axis=-1, keepdims=True)
            halves.append((x * lax.rsqrt(square + EPSILON) * gain).astype(bf16))
        normed = jnp.concatenate(halves, axis=0)
        kv = pack_lanes(wide(normed, wv_ref), wide(normed, wk_ref)).astype(bf16)
        kv_ref[2 * start : 2 * (start + part), :] = kv
        q = wide(normed, wq_ref) * SCALE
        q_ref[start : start + part, :] = pack_lanes(q[:part], q[part:]).astype(bf16)


def project(sequence, gain, wq, wk, wv):
    rows, feat = sequence.shape
    steps = 2
    tile = rows // 2 // steps
    whole = lambda a: pl.BlockSpec(a.shape, lambda t: (0, 0))
    gain = gain.reshape(1, feat)
    wq, wk, wv = wq.T, wk.T, wv.T
    return pl.pallas_call(
        project_kernel,
        grid=(steps,),
        in_specs=[
            pl.BlockSpec((tile, feat), lambda t: (t, 0)),
            pl.BlockSpec((tile, feat), lambda t: (t + steps, 0)),
            whole(gain),
            whole(wq),
            whole(wk),
            whole(wv),
        ],
        out_specs=[
            pl.BlockSpec((2 * tile, 2 * HEAD), lambda t: (t, 0)),
            pl.BlockSpec((tile, 2 * HEAD), lambda t: (t, 0)),
            pl.BlockSpec((tile // POOL, feat), lambda t: (t, 0)),
            pl.BlockSpec((tile // POOL, feat), lambda t: (t, 0)),
        ],
        out_shape=[
            jax.ShapeDtypeStruct((rows, 2 * HEAD), bf16),
            jax.ShapeDtypeStruct((rows // 2, 2 * HEAD), bf16),
            jax.ShapeDtypeStruct((rows // 2 // POOL, feat), f32),
            jax.ShapeDtypeStruct((rows // 2 // POOL, feat), f32),
        ],
        compiler_params=params(),
        name="project",
        cost_estimate=pl.CostEstimate(flops=2 * rows * feat * 3 * HEAD, bytes_accessed=6_000_000, transcendentals=0),
    )(sequence, sequence, gain, wq, wk, wv)


SUB = 256
CHUNK = 1024


def log_rows(logs):
    rows = []
    for log in logs:
        for g in range(log.shape[0] // 128):
            block = jnp.broadcast_to(log[g * 128 : (g + 1) * 128], (128, 128))
            rows.append(block.T[:1])
    return jnp.concatenate(rows, axis=0)


def attend_kernel(*refs, sizes, carried, mode):
    count = len(sizes)
    q_hbm = refs[0]
    kv_hbm = refs[1 : 1 + count]
    rest = list(refs[1 + count :])
    state_hbm = rest.pop(0) if carried else None
    out_hbm = rest.pop(0)
    log_hbm = rest.pop(0) if mode == "final" else None
    q_buf, kv_buf, v_buf, state_buf, out_buf, log_buf, sems = rest
    q_copy = pltpu.make_async_copy(q_hbm, q_buf, sems.at[0])
    q_copy.start()
    copies = []
    at = 0
    for n, (ref, size) in enumerate(zip(kv_hbm, sizes)):
        copy = pltpu.make_async_copy(ref, kv_buf.at[pl.ds(at, size)], sems.at[7 + n])
        copy.start()
        copies.append((at, size, copy))
        at += size
    keys = at
    if carried:
        state_copy = pltpu.make_async_copy(state_hbm, state_buf, sems.at[1])
        state_copy.start()
    q_copy.wait()
    queries = unpack_query(q_buf[...])
    subs = queries.shape[0] // SUB
    chunks = keys // CHUNK
    half = subs // 2
    order = range(subs) if mode == "state" else [i + s * half for i in range(half) for s in range(2)]
    units = [(i, c) for i in order for c in range(chunks)]
    out_copies = []

    def store(rows):
        part = pl.ds(rows[0], rows[1])
        copy = pltpu.make_async_copy(out_buf.at[part], out_hbm.at[part], sems.at[2 + len(out_copies)])
        copy.start()
        out_copies.append(copy)

    def score(unit):
        i, c = unit
        if i == 0:
            for at, size, copy in copies:
                if c * CHUNK <= at < (c + 1) * CHUNK:
                    copy.wait()
            v = kv_buf[c * CHUNK : (c + 1) * CHUNK, :256]
            lane = lanes_of(v.shape)
            v_buf[c * CHUNK : (c + 1) * CHUNK, :] = jnp.where(
                lane < HEAD, v, jnp.where(lane == HEAD, 1.0, 0.0).astype(bf16)
            )
        return lax.dot_general(
            queries[i * SUB : (i + 1) * SUB],
            kv_buf[c * CHUNK : (c + 1) * CHUNK, 128:],
            (((1,), (1,)), ((), ())),
            preferred_element_type=f32,
        )

    following = score(units[0])
    results = {}
    top = total = None
    for n, (i, c) in enumerate(units):
        scores = following
        if n + 1 < len(units):
            following = score(units[n + 1])
        here = jnp.max(scores, axis=1, keepdims=True)
        new = here if c == 0 else jnp.maximum(top, here)
        weights = jnp.exp2(scores - new).astype(bf16)
        mixed = jnp.dot(weights, v_buf[c * CHUNK : (c + 1) * CHUNK, :], preferred_element_type=f32)
        total = mixed if c == 0 else total * jnp.exp2(top - new) + mixed
        top = new
        if c < chunks - 1:
            continue
        if carried:
            if i == 0:
                state_copy.wait()
            before = state_buf[i * SUB : (i + 1) * SUB, :]
            old = before[:, HEAD + 1 : HEAD + 2]
            new = jnp.maximum(top, old)
            total = total * jnp.exp2(top - new) + before * jnp.exp2(old - new)
            top = new
        if mode == "state":
            out_buf[i * SUB : (i + 1) * SUB, :] = jnp.where(lanes_of(total.shape) == HEAD + 1, top, total)
            store((i * SUB, SUB))
            continue
        sums = total[:, HEAD : HEAD + 1]
        results[i] = (total * (1.0 / sums), top + jnp.log2(sums))
        if i >= half:
            packed = pack_lanes(results[i - half][0], results[i][0])
            out_buf[(i - half) * SUB : (i - half + 1) * SUB, :] = packed.astype(out_buf.dtype)
            store(((i - half) * SUB, SUB))
    if mode != "state":
        rows = log_rows([results[i][1] for i in range(subs)])
    if mode == "remote":
        rows = jnp.concatenate([rows, jnp.zeros((16 - rows.shape[0], 128), f32)], axis=0)
        first = rows.astype(bf16)
        left = rows - first.astype(f32)
        second = left.astype(bf16)
        third = (left - second.astype(f32)).astype(bf16)
        out_buf[half * SUB :, :] = jnp.concatenate([first, second, third], axis=1)
        store((half * SUB, 16))
    if mode == "final":
        log_buf[...] = rows
        copy = pltpu.make_async_copy(log_buf, log_hbm, sems.at[6])
        copy.start()
        out_copies.append(copy)
    for copy in out_copies:
        copy.wait()


def attend(query, kvs, state=None, mode="state"):
    rows = query.shape[0]
    sizes = tuple(kv.shape[0] for kv in kvs)
    keys = sum(sizes)
    args = [query, *kvs] + ([] if state is None else [state])
    out_shape = {
        "state": [jax.ShapeDtypeStruct((2 * rows, 256), f32)],
        "remote": [jax.ShapeDtypeStruct((rows + 16, 2 * HEAD), bf16)],
        "final": [
            jax.ShapeDtypeStruct((rows, 2 * HEAD), f32),
            jax.ShapeDtypeStruct((2 * rows // 128, 128), f32),
        ],
    }[mode]
    hbm = pl.BlockSpec(memory_space=pl.ANY)
    out = pl.pallas_call(
        functools.partial(attend_kernel, sizes=sizes, carried=state is not None, mode=mode),
        in_specs=[hbm] * len(args),
        out_specs=[hbm] * len(out_shape),
        out_shape=out_shape,
        scratch_shapes=[
            pltpu.VMEM(query.shape, bf16),
            pltpu.VMEM((keys, 2 * HEAD), bf16),
            pltpu.VMEM((keys, 256), bf16),
            pltpu.VMEM((2 * rows if state is not None else 8, 256), f32),
            pltpu.VMEM(out_shape[0].shape, out_shape[0].dtype),
            pltpu.VMEM((8, 128), f32),
            pltpu.SemaphoreType.DMA((7 + len(kvs),)),
        ],
        compiler_params=params(36 * 2**20),
        name="attend_" + mode,
        cost_estimate=pl.CostEstimate(
            flops=2 * 2 * rows * keys * 512, bytes_accessed=4_000_000, transcendentals=2 * rows * keys
        ),
    )(*args)
    return out if mode == "final" else out[0]


def cut_kernel(below_ref, above_ref, order_ref, out_low_ref, out_high_ref, sems):
    n = out_low_ref.shape[0]
    low = pltpu.make_async_copy(below_ref.at[pl.ds(0, n)], out_low_ref, sems.at[0])
    high = pltpu.make_async_copy(above_ref.at[pl.ds(n, n)], out_high_ref, sems.at[1])
    low.start()
    high.start()
    low.wait()
    high.wait()


def cut(below, above, order):
    hbm = pl.BlockSpec(memory_space=pl.ANY)
    part = jax.ShapeDtypeStruct((below.shape[0] // 2, below.shape[1]), below.dtype)
    return pl.pallas_call(
        cut_kernel,
        in_specs=[hbm] * 3,
        out_specs=[hbm] * 2,
        out_shape=[part] * 2,
        scratch_shapes=[pltpu.SemaphoreType.DMA((2,))],
        compiler_params=params(2**20),
        name="cut",
    )(below, above, order)


def join_kernel(low_ref, high_ref, order_ref, out_ref, sems):
    n = low_ref.shape[0]
    low = pltpu.make_async_copy(low_ref, out_ref.at[pl.ds(0, n)], sems.at[0])
    high = pltpu.make_async_copy(high_ref, out_ref.at[pl.ds(n, n)], sems.at[1])
    low.start()
    high.start()
    low.wait()
    high.wait()


def join(low, high, order):
    hbm = pl.BlockSpec(memory_space=pl.ANY)
    return pl.pallas_call(
        join_kernel,
        in_specs=[hbm] * 3,
        out_specs=hbm,
        out_shape=jax.ShapeDtypeStruct((2 * low.shape[0], low.shape[1]), low.dtype),
        scratch_shapes=[pltpu.SemaphoreType.DMA((2,))],
        compiler_params=params(2**20),
        name="join",
    )(low, high, order)


def relay_kernel(x_ref, order_ref, out_ref, sem):
    copy = pltpu.make_async_copy(x_ref, out_ref, sem)
    copy.start()
    copy.wait()


def relay(x, order):
    hbm = pl.BlockSpec(memory_space=pl.ANY)
    return pl.pallas_call(
        relay_kernel,
        in_specs=[hbm] * 2,
        out_specs=hbm,
        out_shape=jax.ShapeDtypeStruct(x.shape, x.dtype),
        scratch_shapes=[pltpu.SemaphoreType.DMA],
        compiler_params=params(2**20),
        name="relay",
    )(x, order)


def merge_kernel(mine_ref, log_ref, other_ref, out_ref, pool_ref):
    n = out_ref.shape[0]
    stats = other_ref[n:, :].astype(f32)
    rows = (stats[:, :128] + stats[:, 128:256] + stats[:, 256:])[: 2 * n // 128]
    share = 1.0 / (1.0 + jnp.exp2(log_ref[...] - rows))
    columns = []
    for g in range(2 * n // 128):
        columns.append(jnp.broadcast_to(share[g : g + 1], (128, 128)).T)
    low = jnp.concatenate(columns[: n // 128], axis=0)
    high = jnp.concatenate(columns[n // 128 :], axis=0)
    middle = jnp.where(lanes_of(low.shape) < 64, low, high)
    share = jnp.concatenate([low, middle, high], axis=1)
    mine = mine_ref[...]
    attended = (mine + share * (other_ref[:n, :].astype(f32) - mine)).astype(bf16)
    out_ref[...] = attended
    wide = attended.astype(f32)
    pool_ref[...] = jnp.mean(wide.reshape(n // POOL, POOL, wide.shape[1]), axis=1).astype(bf16)


def merge(mine, log, other):
    rows = mine.shape[0]
    vmem = pl.BlockSpec(memory_space=pltpu.VMEM)
    return pl.pallas_call(
        merge_kernel,
        in_specs=[vmem] * 3,
        out_specs=[vmem] * 2,
        out_shape=[
            jax.ShapeDtypeStruct((rows, 2 * HEAD), bf16),
            jax.ShapeDtypeStruct((rows // POOL, 2 * HEAD), bf16),
        ],
        compiler_params=params(16 * 2**20),
        name="merge",
    )(mine, log, other)


def features_kernel(place_ref, *refs):
    pools = refs[:8]
    ml_ref, mh_ref, w_hbm, gain_ref, row_ref, col_ref, attended_hbm = refs[8:15]
    rout_ref, cout_ref, first_ref, last_ref, edge_ref, passed_hbm, pool_buf, w_ref, sems = refs[15:]
    parts = 2
    depth = w_ref.shape[0] // parts
    w_copies = []
    for p in range(parts):
        piece = pl.ds(p * depth, depth)
        w_copies.append(pltpu.make_async_copy(w_hbm.at[piece], w_ref.at[piece], sems.at[p]))
        w_copies[p].start()
    pass_copy = pltpu.make_async_copy(attended_hbm, passed_hbm, sems.at[parts])
    pass_copy.start()
    for k in range(8):
        packed = pools[k][...].astype(f32)
        n = packed.shape[0]
        head = lax.rem(place_ref[1] + 8 - k, 8)
        pool_buf[head, :n] = packed[:, :256]
        pool_buf[head, n:] = pltpu.roll(packed[:, 128:], 192, axis=1)
    part = jnp.concatenate([pool_buf[h][:, :HEAD] for h in range(8)], axis=1)
    lhs = part.astype(bf16)
    both = None
    for p in range(parts):
        w_copies[p].wait()
        piece = slice(p * depth, (p + 1) * depth)
        got = jnp.dot(lhs[:, piece], w_ref[piece, :], preferred_element_type=f32)
        both = got if both is None else both + got
    pooled = jnp.concatenate([ml_ref[...], mh_ref[...]], axis=0) + both
    inverse = lax.rsqrt(jnp.mean(pooled * pooled, axis=-1, keepdims=True) + EPSILON)
    scaled = (pooled * gain_ref[...].astype(f32)).astype(bf16)
    weights = jnp.concatenate([row_ref[...], col_ref[...]], axis=1)
    got = (inverse * jnp.dot(scaled, weights, preferred_element_type=f32)).astype(bf16).astype(f32)
    channels = rout_ref.shape[1]
    row, col = got[:, :channels], got[:, channels:]
    rout_ref[...] = row.astype(bf16)
    cout_ref[...] = col.astype(bf16)
    first_ref[...] = row[:8].astype(bf16)
    last_ref[...] = row[-8:].astype(bf16)
    odd = lax.rem(place_ref[0], 2) == 1
    edge_ref[...] = jnp.where(odd, col[-8:], col[:8]).astype(bf16)
    pass_copy.wait()


def features(place, pools, mean_low, mean_high, out_weight, gain, row_weight, column_weight, attended):
    rows = 2 * mean_low.shape[0]
    channels = row_weight.shape[1]
    vmem = pl.BlockSpec(memory_space=pltpu.VMEM)
    hbm = pl.BlockSpec(memory_space=pl.ANY)
    return pl.pallas_call(
        features_kernel,
        in_specs=[pl.BlockSpec(memory_space=pltpu.SMEM)] + [vmem] * 10 + [hbm] + [vmem] * 3 + [hbm],
        out_specs=[vmem] * 5 + [hbm],
        out_shape=[jax.ShapeDtypeStruct((rows, channels), bf16)] * 2
        + [jax.ShapeDtypeStruct((8, channels), bf16)] * 3
        + [jax.ShapeDtypeStruct(attended.shape, attended.dtype)],
        scratch_shapes=[
            pltpu.VMEM((8, rows, 256), f32),
            pltpu.VMEM(out_weight.shape, bf16),
            pltpu.SemaphoreType.DMA((3,)),
        ],
        compiler_params=params(24 * 2**20),
        name="features",
    )(place, *pools, mean_low, mean_high, out_weight, gain.reshape(1, -1), row_weight, column_weight, attended)


def pair_kernel(
    place_ref, row_ref, row_low_ref, row_high_ref, c0_ref, c1_ref, e0_ref, e1_ref,
    near_ref, far_ref, gain_ref, in_ref, tout_ref,
    out_ref, row_buf, col_buf, wn_ref, wf_ref, xn_ref, xf_ref, first_ref, second_ref,
):
    rows, cols, channels = out_ref.shape
    ctx, col = place_ref[0], place_ref[1]
    gone = jnp.full((8, channels), OUTSIDE, f32)
    row_buf[:8] = jnp.where(ctx == 0, gone, row_low_ref[...].astype(f32))
    row_buf[8 : 8 + rows] = row_ref[...].astype(f32)
    row_buf[8 + rows :] = jnp.where(ctx == 15, gone, row_high_ref[...].astype(f32))
    early = ctx < 8
    c0, c1 = c0_ref[...].astype(f32), c1_ref[...].astype(f32)
    e0, e1 = e0_ref[...].astype(f32), e1_ref[...].astype(f32)
    half = cols // 2
    col_buf[:8] = jnp.where(col == 0, gone, jnp.where(early, e1, e0))
    col_buf[8 : 8 + half] = jnp.where(early, c0, c1)
    col_buf[8 + half : 8 + cols] = jnp.where(early, c1, c0)
    col_buf[8 + cols :] = jnp.where(col == 7, gone, jnp.where(early, e0, e1))

    blank = jnp.zeros((channels, channels), bf16)
    for kernel_ref, w_ref in ((near_ref, wn_ref), (far_ref, wf_ref)):
        for a in range(4):
            for b in range(3):
                at = (a * 3 + b) * channels
                w_ref[at : at + channels, :channels] = kernel_ref[a, b] if a < 3 else blank
                w_ref[at : at + channels, channels:] = kernel_ref[a - 1, b] if a > 0 else blank

    span = cols + 8
    shifted = [col_buf[2 + 2 * b : 2 + 2 * b + span, :] for b in range(3)]
    taps = jnp.concatenate(shifted, axis=1)

    def fill(r):
        row = row_buf[pl.ds(r + 2, 1), :]
        triple = jnp.concatenate([row, row, row], axis=1)
        xn_ref[r] = jnp.maximum(triple + taps, 0.0).astype(bf16)

    def near_step(g):
        start = g * 8
        lhs = []
        for k in (0, 1, 4, 5):
            lhs.append(jnp.concatenate([xn_ref[start + k + 2 * a] for a in range(4)], axis=1))
        got = jnp.dot(jnp.concatenate(lhs, axis=0), wn_ref[...], preferred_element_type=f32)
        for n, k in enumerate((0, 1, 4, 5)):
            for side in range(2):
                r = start + k + 2 * side
                part = got[n * span : (n + 1) * span, side * channels : (side + 1) * channels]
                first = part + row_buf[pl.ds(r + 4, 1), :] + shifted[1]
                centre = first[4 : 4 + cols]
                first_ref[r] = centre
                hidden = jnp.concatenate([first[:cols], centre, first[8 : 8 + cols]], axis=1)
                xf_ref[r] = jnp.maximum(hidden, 0.0).astype(bf16)

    def far_step(g):
        start = g * 8
        lhs = []
        for k in range(4):
            lhs.append(jnp.concatenate([xf_ref[start + k + 4 * a] for a in range(4)], axis=1))
        got = jnp.dot(jnp.concatenate(lhs, axis=0), wf_ref[...], preferred_element_type=f32)
        for side in range(2):
            for k in range(4):
                part = got[k * cols : (k + 1) * cols, side * channels : (side + 1) * channels]
                second_ref[4 * side + k] = part + first_ref[start + 4 * side + k + 4]

    def transition_step(g):
        start = g * 8
        second = second_ref[...].reshape(8 * cols, channels)
        centred = second - jnp.mean(second, axis=-1, keepdims=True)
        variance = jnp.mean(centred * centred, axis=-1, keepdims=True)
        layer = (centred * lax.rsqrt(variance + LAYER_EPSILON) * gain_ref[...].astype(f32)).astype(bf16)
        middle = jnp.dot(layer, in_ref[...], preferred_element_type=f32)
        middle = jnp.maximum(middle, 0.0).astype(bf16)
        result = (second + jnp.dot(middle, tout_ref[...], preferred_element_type=f32)).astype(bf16)
        for k in range(8):
            out_ref[start + k] = result[k * cols : (k + 1) * cols]

    last = rows // 8
    for r in range(12):
        fill(r)

    def fill_for(g):
        for r in range(8):
            fill(g * 8 + 4 + r)

    near_step(0)
    fill_for(1)
    near_step(1)
    fill_for(2)
    far_step(0)
    near_step(2)
    fill_for(3)

    def steady(g, carry):
        transition_step(g - 3)
        far_step(g - 2)
        near_step(g)

        @pl.when(g < last)
        def _():
            fill_for(g + 1)

        return carry

    lax.fori_loop(3, last + 1, steady, 0)
    transition_step(last - 2)
    far_step(last - 1)
    transition_step(last - 1)


def pair_map(place, row, row_low, row_high, blocks, edges, near, far, gain, trans_in, trans_out):
    rows, channels = row.shape
    cols = 2 * blocks[0].shape[0]
    vmem = pl.BlockSpec(memory_space=pltpu.VMEM)
    return pl.pallas_call(
        pair_kernel,
        in_specs=[pl.BlockSpec(memory_space=pltpu.SMEM)] + [vmem] * 12,
        out_specs=vmem,
        out_shape=jax.ShapeDtypeStruct((rows, cols, channels), bf16),
        scratch_shapes=[
            pltpu.VMEM((rows + 16, channels), f32),
            pltpu.VMEM((cols + 16, channels), f32),
            pltpu.VMEM((12 * channels, 2 * channels), bf16),
            pltpu.VMEM((12 * channels, 2 * channels), bf16),
            pltpu.VMEM((rows + 12, cols + 8, 3 * channels), bf16),
            pltpu.VMEM((rows + 8, cols, 3 * channels), bf16),
            pltpu.VMEM((rows + 8, cols, channels), f32),
            pltpu.VMEM((8, cols, channels), f32),
        ],
        compiler_params=params(),
        name="pair_map",
        cost_estimate=pl.CostEstimate(flops=14_000_000_000, bytes_accessed=3_000_000, transcendentals=0),
    )(place, row, row_low, row_high, *blocks, *edges, near, far, gain.reshape(1, -1), trans_in, trans_out)


def trunk_kernel(place_ref, near_hbm, far_hbm, seq_hbm, w_hbm, out_ref, all_buf, seq_buf, wl_buf, wh_buf, turned, sems):
    n = all_buf.shape[1]
    base = pl.multiple_of((place_ref[1] * 3 // 2) * 128, 128)
    window = pl.ds(base, 256)
    copies = [[pltpu.make_async_copy(seq_hbm.at[:, window], seq_buf, sems.at[0])]]
    for h in range(8):
        ref = near_hbm if h < 4 else far_hbm
        group = lax.rem(place_ref[1] // 4 + h // 4, 2)
        row = pl.multiple_of((group * 4 + h % 4) * HEAD, HEAD)
        weight = w_hbm.at[pl.ds(row, HEAD), window]
        copies.append(
            [
                pltpu.make_async_copy(ref.at[pl.ds(h % 4 * n, n)], all_buf.at[h], sems.at[1 + 3 * h]),
                pltpu.make_async_copy(weight, wl_buf.at[pl.ds(h * 256, HEAD)], sems.at[2 + 3 * h]),
                pltpu.make_async_copy(weight, wh_buf.at[pl.ds(h * 256 + 64, HEAD)], sems.at[3 + 3 * h]),
            ]
        )
    for group in copies:
        for copy in group:
            copy.start()
    for h in range(8):
        wl_buf[h * 256 + HEAD : (h + 1) * 256, :] = jnp.zeros((64, 256), bf16)
        wh_buf[h * 256 : h * 256 + 64, :] = jnp.zeros((64, 256), bf16)
    copies[0][0].wait()
    parts = [seq_buf[side * n : (side + 1) * n, :].astype(f32) for side in range(2)]
    for h in (0, 4):
        for group in copies[1 + h : 5 + h]:
            for copy in group:
                copy.wait()
        for side, w_buf in ((0, wl_buf), (1, wh_buf)):
            lhs = jnp.concatenate([all_buf[h + k][:, 128 * side : 128 * side + 256] for k in range(4)], axis=1)
            weight = w_buf[h * 256 : (h + 4) * 256, :]
            parts[side] = parts[side] + jnp.dot(lhs, weight, preferred_element_type=f32)
    for side in range(2):
        turned[:, side * n : (side + 1) * n] = parts[side].T
    offset = pl.multiple_of(lax.rem(place_ref[1], 2) * 64, 64)
    out_ref[...] = turned[pl.ds(offset, HEAD), :].astype(bf16)


def trunk(place, near, far, sequence, out_weight):
    vmem = pl.BlockSpec(memory_space=pltpu.VMEM)
    hbm = pl.BlockSpec(memory_space=pl.ANY)
    rows = sequence.shape[0]
    turned = pl.pallas_call(
        trunk_kernel,
        in_specs=[pl.BlockSpec(memory_space=pltpu.SMEM)] + [hbm] * 4,
        out_specs=vmem,
        out_shape=jax.ShapeDtypeStruct((HEAD, rows), bf16),
        scratch_shapes=[
            pltpu.VMEM((8, rows // 2, 2 * HEAD), bf16),
            pltpu.VMEM((rows, 256), bf16),
            pltpu.VMEM((8 * 256, 256), bf16),
            pltpu.VMEM((8 * 256, 256), bf16),
            pltpu.VMEM((256, rows), f32),
            pltpu.SemaphoreType.DMA((25,)),
        ],
        compiler_params=params(),
        name="trunk",
        cost_estimate=pl.CostEstimate(flops=700_000_000, bytes_accessed=5_000_000, transcendentals=0),
    )(place, near, far, sequence, out_weight)
    return turned.T


def per_device(
    sequence,
    norm_gain,
    query_weight,
    key_weight,
    value_weight,
    out_weight,
    pool_gain,
    row_weight,
    column_weight,
    conv_near,
    conv_far,
    trans_gain,
    trans_in,
    trans_out,
):
    place = jnp.stack([lax.axis_index("ctx"), lax.axis_index("col")]).astype(jnp.int32)
    spots = range(16)
    cols = range(8)
    to_core = [(i, i ^ 1) for i in spots]
    to_z = [(i, i ^ 8) for i in spots]
    to_up = [(i, (i & 8) | ((i + 2) & 7)) for i in spots]
    to_down = [(i, (i & 8) | ((i - 2) & 7)) for i in spots]

    def send(x, perm):
        return lax.ppermute(x, "ctx", perm)

    kv, query, mean_low, mean_high = project(sequence, norm_gain, query_weight, key_weight, value_weight)
    kv_below = send(kv, to_up)
    kv_above = send(kv, to_down)
    query_z = send(query, to_z)
    kv_core = send(kv, to_core)
    state = attend(query, [kv])
    low, high = cut(kv_below, kv_above, state)
    far_below = send(low, to_up)
    far_above = send(high, to_down)
    twin = [kv_core, send(kv_below, to_core), send(kv_above, to_core)]
    state_z = attend(query_z, [kv, kv_below, kv_above])
    opposite = join(far_below, far_above, state_z)
    opposite_core = send(opposite, to_core)
    state_z = attend(query_z, twin, state_z)
    returned = attend(query_z, [opposite, opposite_core], state_z, mode="remote")
    other = send(returned, to_z)
    rest = [kv_below, kv_above, *twin, opposite, opposite_core]
    mine, log = attend(query, rest, state, mode="final")
    attended, pool = merge(mine, log, other)

    pools = [pool] + [lax.ppermute(pool, "col", [(i, (i + k) % 8) for i in cols]) for k in range(1, 8)]
    along_y = [[0, 1, 2, 3], [4, 5, 6, 7]]
    near_heads = lax.all_gather(attended, "col", axis=0, tiled=True, axis_index_groups=along_y)
    row, column, first_rows, last_rows, edge, attended = features(
        place, pools, mean_low, mean_high, out_weight, pool_gain, row_weight, column_weight, attended
    )
    attended_z = lax.ppermute(attended, "col", [(i, i ^ 4) for i in cols])

    row_low = lax.ppermute(last_rows, "ctx", [(i, i + 1) for i in range(15)])
    row_high = lax.ppermute(first_rows, "ctx", [(i + 1, i) for i in range(15)])
    blocks, edges = [], []
    for turn_no in range(2):
        whole_perm, edge_perm = [], []
        for j in spots:
            for s in cols:
                i = s + 8 * (turn_no if j % 2 == 0 else 1 - turn_no)
                whole_perm.append((j * 8 + s, i * 8 + j // 2))
                target = (j + 1) // 2 if j % 2 == 1 else (j - 2) // 2
                if 0 <= target < 8:
                    edge_perm.append((j * 8 + s, i * 8 + target))
        blocks.append(lax.ppermute(column, ("ctx", "col"), whole_perm))
        edges.append(lax.ppermute(edge, ("ctx", "col"), edge_perm))
    attended_z = relay(attended_z, edges[1])
    far_heads = lax.all_gather(attended_z, "col", axis=0, tiled=True, axis_index_groups=along_y)
    pair_out = pair_map(
        place, row, row_low, row_high, blocks, edges, conv_near, conv_far, trans_gain, trans_in, trans_out
    )
    trunk_out = trunk(place, near_heads, far_heads, sequence, out_weight)
    return (trunk_out, pair_out)


def solution(mesh):
    return jax.shard_map(
        per_device,
        mesh=mesh,
        in_specs=(
            P("ctx", None),
            P(),
            P(None, "col"),
            P(None, "col"),
            P(None, "col"),
            P(),
            P(),
            P(),
            P(),
            P(),
            P(),
            P(),
            P(),
            P(),
        ),
        out_specs=(P("ctx", "col"), P("ctx", "col", None)),
        check_vma=False,
    )
```

```python
import functools
import math

import jax
import jax.numpy as jnp
from jax import lax
from jax.experimental import pallas as pl
from jax.experimental.pallas import tpu as pltpu
from jax.sharding import PartitionSpec as P

POOL = 16
HEAD = 192
EPSILON = 1e-06
LAYER_EPSILON = 1e-05
OUTSIDE = -1e30
SCALE = math.log2(math.e) / math.sqrt(HEAD)
bf16 = jnp.bfloat16
f32 = jnp.float32
VMEM = 56 * 2**20


def params(limit=VMEM):
    return pltpu.CompilerParams(vmem_limit_bytes=limit)


def lanes_of(shape):
    return lax.broadcasted_iota(jnp.int32, shape, len(shape) - 1)


def pack_lanes(low, high):
    rolled = pltpu.roll(high, 64, axis=1)
    middle = jnp.where(lanes_of(rolled.shape) < 64, pltpu.roll(low, 128, axis=1), rolled)
    return jnp.concatenate([low[:, :128], middle], axis=1)


def unpack_query(packed):
    wide = pltpu.roll(packed[:, :256].astype(f32), 64, axis=1)
    lane = lanes_of(wide.shape)
    low = jnp.where(lane < 64, 0.0, wide).astype(bf16)
    high = jnp.where(lane < 64, 0.0, packed[:, 128:].astype(f32)).astype(bf16)
    return jnp.concatenate([low, high], axis=0)


def project_kernel(low_ref, high_ref, gain_ref, wq_ref, wk_ref, wv_ref, kv_ref, q_ref, ml_ref, mh_ref):
    gain = gain_ref[...].astype(f32).reshape(1, -1)
    rows = low_ref.shape[0]
    part = rows // 2

    def wide(normed, w_ref):
        y = lax.dot_general(normed, w_ref[...], (((1,), (1,)), ((), ())), preferred_element_type=f32)
        return jnp.concatenate([y, jnp.zeros((y.shape[0], 64), f32)], axis=1)

    for start in range(0, rows, part):
        halves = []
        for ref, mean_ref in ((low_ref, ml_ref), (high_ref, mh_ref)):
            x = ref[start : start + part, :].astype(f32)
            mean = jnp.mean(x.reshape(part // POOL, POOL, x.shape[1]), axis=1)
            mean_ref[start // POOL : (start + part) // POOL, :] = mean
            square = jnp.mean(x * x, axis=-1, keepdims=True)
            halves.append((x * lax.rsqrt(square + EPSILON) * gain).astype(bf16))
        normed = jnp.concatenate(halves, axis=0)
        kv = pack_lanes(wide(normed, wv_ref), wide(normed, wk_ref)).astype(bf16)
        kv_ref[2 * start : 2 * (start + part), :] = kv
        q = wide(normed, wq_ref) * SCALE
        q_ref[start : start + part, :] = pack_lanes(q[:part], q[part:]).astype(bf16)


def project(sequence, gain, wq, wk, wv):
    rows, feat = sequence.shape
    steps = 2
    tile = rows // 2 // steps
    whole = lambda a: pl.BlockSpec(a.shape, lambda t: (0, 0))
    wq, wk, wv = wq.T, wk.T, wv.T
    return pl.pallas_call(
        project_kernel,
        grid=(steps,),
        in_specs=[
            pl.BlockSpec((tile, feat), lambda t: (t, 0)),
            pl.BlockSpec((tile, feat), lambda t: (t + steps, 0)),
            pl.BlockSpec(gain.shape, lambda t: (0,)),
            whole(wq),
            whole(wk),
            whole(wv),
        ],
        out_specs=[
            pl.BlockSpec((2 * tile, 2 * HEAD), lambda t: (t, 0)),
            pl.BlockSpec((tile, 2 * HEAD), lambda t: (t, 0)),
            pl.BlockSpec((tile // POOL, feat), lambda t: (t, 0)),
            pl.BlockSpec((tile // POOL, feat), lambda t: (t, 0)),
        ],
        out_shape=[
            jax.ShapeDtypeStruct((rows, 2 * HEAD), bf16),
            jax.ShapeDtypeStruct((rows // 2, 2 * HEAD), bf16),
            jax.ShapeDtypeStruct((rows // 2 // POOL, feat), f32),
            jax.ShapeDtypeStruct((rows // 2 // POOL, feat), f32),
        ],
        compiler_params=params(),
        name="project",
        cost_estimate=pl.CostEstimate(flops=2 * rows * feat * 3 * HEAD, bytes_accessed=6_000_000, transcendentals=0),
    )(sequence, sequence, gain, wq, wk, wv)


SUB = 256
CHUNK = 1024


def log_rows(logs):
    rows = []
    for log in logs:
        for g in range(log.shape[0] // 128):
            block = jnp.broadcast_to(log[g * 128 : (g + 1) * 128], (128, 128))
            rows.append(block.T[:1])
    return jnp.concatenate(rows, axis=0)


def attend_kernel(*refs, sizes, carried, mode, orders):
    count = len(sizes)
    q_hbm = refs[0]
    kv_hbm = refs[1 : 1 + count]
    rest = list(refs[1 + count :])
    state_hbm = rest.pop(0) if carried else None
    rest = rest[orders:]
    out_hbm = rest.pop(0)
    log_hbm = rest.pop(0) if mode == "final" else None
    q_buf, kv_buf, v_buf, state_buf, out_buf, log_buf, sems = rest
    q_copy = pltpu.make_async_copy(q_hbm, q_buf, sems.at[0])
    q_copy.start()
    copies = []
    at = 0
    for n, (ref, size) in enumerate(zip(kv_hbm, sizes)):
        copy = pltpu.make_async_copy(ref, kv_buf.at[pl.ds(at, size)], sems.at[7 + n])
        copy.start()
        copies.append((at, size, copy))
        at += size
    keys = at
    if carried:
        state_copy = pltpu.make_async_copy(state_hbm, state_buf, sems.at[1])
        state_copy.start()
    q_copy.wait()
    queries = unpack_query(q_buf[...])
    subs = queries.shape[0] // SUB
    chunks = keys // CHUNK
    half = subs // 2
    order = range(subs) if mode == "state" else [i + s * half for i in range(half) for s in range(2)]
    units = [(i, c) for i in order for c in range(chunks)]
    out_copies = []

    def store(rows):
        part = pl.ds(rows[0], rows[1])
        copy = pltpu.make_async_copy(out_buf.at[part], out_hbm.at[part], sems.at[2 + len(out_copies)])
        copy.start()
        out_copies.append(copy)

    def score(unit):
        i, c = unit
        if i == 0:
            for at, size, copy in copies:
                if c * CHUNK <= at < (c + 1) * CHUNK:
                    copy.wait()
            v = kv_buf[c * CHUNK : (c + 1) * CHUNK, :256]
            lane = lanes_of(v.shape)
            v_buf[c * CHUNK : (c + 1) * CHUNK, :] = jnp.where(
                lane < HEAD, v, jnp.where(lane == HEAD, 1.0, 0.0).astype(bf16)
            )
        return lax.dot_general(
            queries[i * SUB : (i + 1) * SUB],
            kv_buf[c * CHUNK : (c + 1) * CHUNK, 128:],
            (((1,), (1,)), ((), ())),
            preferred_element_type=f32,
        )

    following = score(units[0])
    results = {}
    top = total = None
    for n, (i, c) in enumerate(units):
        scores = following
        if n + 1 < len(units):
            following = score(units[n + 1])
        here = jnp.max(scores, axis=1, keepdims=True)
        new = here if c == 0 else jnp.maximum(top, here)
        weights = jnp.exp2(scores - new).astype(bf16)
        mixed = jnp.dot(weights, v_buf[c * CHUNK : (c + 1) * CHUNK, :], preferred_element_type=f32)
        total = mixed if c == 0 else total * jnp.exp2(top - new) + mixed
        top = new
        if c < chunks - 1:
            continue
        if carried:
            if i == 0:
                state_copy.wait()
            before = state_buf[i * SUB : (i + 1) * SUB, :]
            old = before[:, HEAD + 1 : HEAD + 2]
            new = jnp.maximum(top, old)
            total = total * jnp.exp2(top - new) + before * jnp.exp2(old - new)
            top = new
        if mode == "state":
            out_buf[i * SUB : (i + 1) * SUB, :] = jnp.where(lanes_of(total.shape) == HEAD + 1, top, total)
            store((i * SUB, SUB))
            continue
        sums = total[:, HEAD : HEAD + 1]
        results[i] = (total * (1.0 / sums), top + jnp.log2(sums))
        if i >= half:
            packed = pack_lanes(results[i - half][0], results[i][0])
            out_buf[(i - half) * SUB : (i - half + 1) * SUB, :] = packed.astype(out_buf.dtype)
            store(((i - half) * SUB, SUB))
    if mode != "state":
        rows = log_rows([results[i][1] for i in range(subs)])
    if mode == "remote":
        rows = jnp.concatenate([rows, jnp.zeros((16 - rows.shape[0], 128), f32)], axis=0)
        first = rows.astype(bf16)
        left = rows - first.astype(f32)
        second = left.astype(bf16)
        third = (left - second.astype(f32)).astype(bf16)
        out_buf[half * SUB :, :] = jnp.concatenate([first, second, third], axis=1)
        store((half * SUB, 16))
    if mode == "final":
        log_buf[...] = rows
        copy = pltpu.make_async_copy(log_buf, log_hbm, sems.at[6])
        copy.start()
        out_copies.append(copy)
    for copy in out_copies:
        copy.wait()


def attend(query, kvs, state=None, mode="state", orders=()):
    rows = query.shape[0]
    sizes = tuple(kv.shape[0] for kv in kvs)
    keys = sum(sizes)
    args = [query, *kvs] + ([] if state is None else [state]) + list(orders)
    out_shape = {
        "state": [jax.ShapeDtypeStruct((2 * rows, 256), f32)],
        "remote": [jax.ShapeDtypeStruct((rows + 16, 2 * HEAD), bf16)],
        "final": [
            jax.ShapeDtypeStruct((rows, 2 * HEAD), f32),
            jax.ShapeDtypeStruct((2 * rows // 128, 128), f32),
        ],
    }[mode]
    hbm = pl.BlockSpec(memory_space=pl.ANY)
    out = pl.pallas_call(
        functools.partial(attend_kernel, sizes=sizes, carried=state is not None, mode=mode, orders=len(orders)),
        in_specs=[hbm] * len(args),
        out_specs=[hbm] * len(out_shape),
        out_shape=out_shape,
        scratch_shapes=[
            pltpu.VMEM(query.shape, bf16),
            pltpu.VMEM((keys, 2 * HEAD), bf16),
            pltpu.VMEM((keys, 256), bf16),
            pltpu.VMEM((2 * rows if state is not None else 8, 256), f32),
            pltpu.VMEM(out_shape[0].shape, out_shape[0].dtype),
            pltpu.VMEM((8, 128), f32),
            pltpu.SemaphoreType.DMA((7 + len(kvs),)),
        ],
        compiler_params=params(36 * 2**20),
        name="attend_" + mode,
        cost_estimate=pl.CostEstimate(
            flops=2 * 2 * rows * keys * 512, bytes_accessed=4_000_000, transcendentals=2 * rows * keys
        ),
    )(*args)
    return out if mode == "final" else out[0]


def cut_kernel(below_ref, above_ref, *refs):
    out_low_ref, out_high_ref, sems = refs[-3:]
    n = out_low_ref.shape[0]
    low = pltpu.make_async_copy(below_ref.at[pl.ds(0, n)], out_low_ref, sems.at[0])
    high = pltpu.make_async_copy(above_ref.at[pl.ds(n, n)], out_high_ref, sems.at[1])
    low.start()
    high.start()
    low.wait()
    high.wait()


def cut(below, above, *orders):
    hbm = pl.BlockSpec(memory_space=pl.ANY)
    part = jax.ShapeDtypeStruct((below.shape[0] // 2, below.shape[1]), below.dtype)
    return pl.pallas_call(
        cut_kernel,
        in_specs=[hbm] * (2 + len(orders)),
        out_specs=[hbm] * 2,
        out_shape=[part] * 2,
        scratch_shapes=[pltpu.SemaphoreType.DMA((2,))],
        compiler_params=params(2**20),
        name="cut",
    )(below, above, *orders)


def join_kernel(low_ref, high_ref, order_ref, out_ref, sems):
    n = low_ref.shape[0]
    low = pltpu.make_async_copy(low_ref, out_ref.at[pl.ds(0, n)], sems.at[0])
    high = pltpu.make_async_copy(high_ref, out_ref.at[pl.ds(n, n)], sems.at[1])
    low.start()
    high.start()
    low.wait()
    high.wait()


def join(low, high, order):
    hbm = pl.BlockSpec(memory_space=pl.ANY)
    return pl.pallas_call(
        join_kernel,
        in_specs=[hbm] * 3,
        out_specs=hbm,
        out_shape=jax.ShapeDtypeStruct((2 * low.shape[0], low.shape[1]), low.dtype),
        scratch_shapes=[pltpu.SemaphoreType.DMA((2,))],
        compiler_params=params(2**20),
        name="join",
    )(low, high, order)


def relay_kernel(x_ref, *refs):
    out_ref, sem = refs[-2:]
    copy = pltpu.make_async_copy(x_ref, out_ref, sem)
    copy.start()
    copy.wait()


def relay(x, *orders):
    hbm = pl.BlockSpec(memory_space=pl.ANY)
    return pl.pallas_call(
        relay_kernel,
        in_specs=[hbm] * (1 + len(orders)),
        out_specs=hbm,
        out_shape=jax.ShapeDtypeStruct(x.shape, x.dtype),
        scratch_shapes=[pltpu.SemaphoreType.DMA],
        compiler_params=params(2**20),
        name="relay",
    )(x, *orders)


def merge_kernel(mine_ref, log_ref, other_ref, out_ref, pool_ref):
    n = out_ref.shape[0]
    stats = other_ref[n:, :].astype(f32)
    rows = (stats[:, :128] + stats[:, 128:256] + stats[:, 256:])[: 2 * n // 128]
    share = 1.0 / (1.0 + jnp.exp2(log_ref[...] - rows))
    columns = []
    for g in range(2 * n // 128):
        columns.append(jnp.broadcast_to(share[g : g + 1], (128, 128)).T)
    low = jnp.concatenate(columns[: n // 128], axis=0)
    high = jnp.concatenate(columns[n // 128 :], axis=0)
    middle = jnp.where(lanes_of(low.shape) < 64, low, high)
    share = jnp.concatenate([low, middle, high], axis=1)
    mine = mine_ref[...]
    attended = (mine + share * (other_ref[:n, :].astype(f32) - mine)).astype(bf16)
    out_ref[...] = attended
    wide = attended.astype(f32)
    pool = jnp.mean(wide.reshape(n // POOL, POOL, wide.shape[1]), axis=1).astype(bf16)
    for k in range(pool_ref.shape[0]):
        pool_ref[k] = pool


def merge(mine, log, other):
    rows = mine.shape[0]
    vmem = pl.BlockSpec(memory_space=pltpu.VMEM)
    return pl.pallas_call(
        merge_kernel,
        in_specs=[vmem] * 3,
        out_specs=[vmem] * 2,
        out_shape=[
            jax.ShapeDtypeStruct((rows, 2 * HEAD), bf16),
            jax.ShapeDtypeStruct((8, rows // POOL, 2 * HEAD), bf16),
        ],
        compiler_params=params(16 * 2**20),
        name="merge",
    )(mine, log, other)


def features_kernel(pool_ref, ml_ref, mh_ref, w_hbm, gain_ref, row_ref, col_ref, rout_ref, sent_ref, w_ref, sems):
    parts = 3
    depth = w_ref.shape[0] // parts
    w_copies = []
    for p in range(parts):
        piece = pl.ds(p * depth, depth)
        w_copies.append(pltpu.make_async_copy(w_hbm.at[piece], w_ref.at[piece], sems.at[p]))
        w_copies[p].start()
    heads = []
    for h in range(8):
        packed = pool_ref[h].astype(f32)
        low, high = packed[:, :256], pltpu.roll(packed[:, 128:], 192, axis=1)
        heads.append(jnp.concatenate([low, high], axis=0)[:, :HEAD])
    lhs = jnp.concatenate(heads, axis=1).astype(bf16)
    pooled = jnp.concatenate([ml_ref[...], mh_ref[...]], axis=0)
    for p in range(parts):
        w_copies[p].wait()
        piece = slice(p * depth, (p + 1) * depth)
        pooled = pooled + jnp.dot(lhs[:, piece], w_ref[piece, :], preferred_element_type=f32)
    inverse = lax.rsqrt(jnp.mean(pooled * pooled, axis=-1, keepdims=True) + EPSILON)
    scaled = (pooled * gain_ref[...].astype(f32)).astype(bf16)
    weights = jnp.concatenate([row_ref[...], col_ref[...]], axis=1)
    got = (inverse * jnp.dot(scaled, weights, preferred_element_type=f32)).astype(bf16).astype(f32)
    channels = rout_ref.shape[1]
    row, col = got[:, :channels], got[:, channels:]
    rout_ref[...] = row.astype(bf16)
    sent = jnp.concatenate([col, row[:8], row[-8:]], axis=0).astype(bf16)
    for k in range(sent_ref.shape[0]):
        sent_ref[k] = sent


def features(pools, mean_low, mean_high, out_weight, gain, row_weight, column_weight, copies):
    rows = 2 * mean_low.shape[0]
    channels = row_weight.shape[1]
    vmem = pl.BlockSpec(memory_space=pltpu.VMEM)
    hbm = pl.BlockSpec(memory_space=pl.ANY)
    return pl.pallas_call(
        features_kernel,
        in_specs=[vmem] * 3 + [hbm] + [vmem] * 3,
        out_specs=[vmem] * 2,
        out_shape=[
            jax.ShapeDtypeStruct((rows, channels), bf16),
            jax.ShapeDtypeStruct((copies, rows + 16, channels), bf16),
        ],
        scratch_shapes=[pltpu.VMEM(out_weight.shape, bf16), pltpu.SemaphoreType.DMA((3,))],
        compiler_params=params(24 * 2**20),
        name="features",
    )(pools, mean_low, mean_high, out_weight, gain, row_weight, column_weight)


def pair_kernel(
    place_ref, row_ref, got_ref, near_ref, far_ref, gain_ref, in_ref, tout_ref, order_ref,
    out_ref, row_buf, col_buf, wn_ref, wf_ref, xn_ref, xf_ref, first_ref, second_ref,
):
    rows, cols, channels = out_ref.shape
    ctx, col = place_ref[0], place_ref[1]
    gone = jnp.full((8, channels), OUTSIDE, f32)
    spots = got_ref.shape[0]
    above = got_ref[jnp.maximum(ctx - 1, 0)][rows + 8 :].astype(f32)
    below = got_ref[jnp.minimum(ctx + 1, spots - 1)][rows : rows + 8].astype(f32)
    row_buf[:8] = jnp.where(ctx == 0, gone, above)
    row_buf[8 : 8 + rows] = row_ref[...].astype(f32)
    row_buf[8 + rows :] = jnp.where(ctx == spots - 1, gone, below)
    half = cols // 2
    left = got_ref[jnp.maximum(2 * col - 1, 0)][half - 8 : half].astype(f32)
    right = got_ref[jnp.minimum(2 * col + 2, spots - 1)][:8].astype(f32)
    col_buf[:8] = jnp.where(col == 0, gone, left)
    col_buf[8 : 8 + half] = got_ref[2 * col][:half].astype(f32)
    col_buf[8 + half : 8 + cols] = got_ref[2 * col + 1][:half].astype(f32)
    col_buf[8 + cols :] = jnp.where(2 * col + 2 >= spots, gone, right)

    blank = jnp.zeros((channels, channels), bf16)
    for kernel_ref, w_ref in ((near_ref, wn_ref), (far_ref, wf_ref)):
        for a in range(4):
            for b in range(3):
                at = (a * 3 + b) * channels
                w_ref[at : at + channels, :channels] = kernel_ref[a, b] if a < 3 else blank
                w_ref[at : at + channels, channels:] = kernel_ref[a - 1, b] if a > 0 else blank

    span = cols + 8
    shifted = [col_buf[2 + 2 * b : 2 + 2 * b + span, :] for b in range(3)]
    taps = jnp.concatenate(shifted, axis=1)

    def fill(r):
        row = row_buf[pl.ds(r + 2, 1), :]
        triple = jnp.concatenate([row, row, row], axis=1)
        xn_ref[r] = jnp.maximum(triple + taps, 0.0).astype(bf16)

    def near_step(g):
        start = g * 8
        lhs = []
        for k in (0, 1, 4, 5):
            lhs.append(jnp.concatenate([xn_ref[start + k + 2 * a] for a in range(4)], axis=1))
        got = jnp.dot(jnp.concatenate(lhs, axis=0), wn_ref[...], preferred_element_type=f32)
        for n, k in enumerate((0, 1, 4, 5)):
            for side in range(2):
                r = start + k + 2 * side
                part = got[n * span : (n + 1) * span, side * channels : (side + 1) * channels]
                first = part + row_buf[pl.ds(r + 4, 1), :] + shifted[1]
                centre = first[4 : 4 + cols]
                first_ref[r] = centre
                hidden = jnp.concatenate([first[:cols], centre, first[8 : 8 + cols]], axis=1)
                xf_ref[r] = jnp.maximum(hidden, 0.0).astype(bf16)

    def far_step(g):
        start = g * 8
        lhs = []
        for k in range(4):
            lhs.append(jnp.concatenate([xf_ref[start + k + 4 * a] for a in range(4)], axis=1))
        got = jnp.dot(jnp.concatenate(lhs, axis=0), wf_ref[...], preferred_element_type=f32)
        for side in range(2):
            for k in range(4):
                part = got[k * cols : (k + 1) * cols, side * channels : (side + 1) * channels]
                second_ref[4 * side + k] = part + first_ref[start + 4 * side + k + 4]

    def transition_step(g):
        start = g * 8
        second = second_ref[...].reshape(8 * cols, channels)
        centred = second - jnp.mean(second, axis=-1, keepdims=True)
        variance = jnp.mean(centred * centred, axis=-1, keepdims=True)
        layer = (centred * lax.rsqrt(variance + LAYER_EPSILON) * gain_ref[...].astype(f32)).astype(bf16)
        middle = jnp.dot(layer, in_ref[...], preferred_element_type=f32)
        middle = jnp.maximum(middle, 0.0).astype(bf16)
        result = (second + jnp.dot(middle, tout_ref[...], preferred_element_type=f32)).astype(bf16)
        for k in range(8):
            out_ref[start + k] = result[k * cols : (k + 1) * cols]

    last = rows // 8
    for r in range(12):
        fill(r)

    def fill_for(g):
        for r in range(8):
            fill(g * 8 + 4 + r)

    near_step(0)
    fill_for(1)
    near_step(1)
    fill_for(2)
    far_step(0)
    near_step(2)
    fill_for(3)

    def steady(g, carry):
        near_step(g)
        transition_step(g - 3)
        far_step(g - 2)

        @pl.when(g < last)
        def _():
            fill_for(g + 1)

        return carry

    lax.fori_loop(3, last + 1, steady, 0)
    transition_step(last - 2)
    far_step(last - 1)
    transition_step(last - 1)


def pair_map(place, row, got, near, far, gain, trans_in, trans_out, order):
    rows, channels = row.shape
    cols = 2 * rows
    vmem = pl.BlockSpec(memory_space=pltpu.VMEM)
    return pl.pallas_call(
        pair_kernel,
        in_specs=[pl.BlockSpec(memory_space=pltpu.SMEM)] + [vmem] * 7 + [pl.BlockSpec(memory_space=pl.ANY)],
        out_specs=vmem,
        out_shape=jax.ShapeDtypeStruct((rows, cols, channels), bf16),
        scratch_shapes=[
            pltpu.VMEM((rows + 16, channels), f32),
            pltpu.VMEM((cols + 16, channels), f32),
            pltpu.VMEM((12 * channels, 2 * channels), bf16),
            pltpu.VMEM((12 * channels, 2 * channels), bf16),
            pltpu.VMEM((rows + 12, cols + 8, 3 * channels), bf16),
            pltpu.VMEM((rows + 8, cols, 3 * channels), bf16),
            pltpu.VMEM((rows + 8, cols, channels), f32),
            pltpu.VMEM((8, cols, channels), f32),
        ],
        compiler_params=params(),
        name="pair_map",
        cost_estimate=pl.CostEstimate(flops=14_000_000_000, bytes_accessed=3_000_000, transcendentals=0),
    )(place, row, got, near, far, gain, trans_in, trans_out, order)


def trunk_kernel(place_ref, near_hbm, seq_hbm, w_hbm, mine_ref, sent_ref, all_buf, seq_buf, wl_buf, wh_buf, turned, sems):
    n = all_buf.shape[1]
    col = place_ref[1]
    other = lax.rem(col + 4, 8)
    windows = [pl.ds(pl.multiple_of((c * 3 // 2) * 128, 128), 256) for c in (col, other)]
    seq_copy = pltpu.make_async_copy(seq_hbm.at[:, windows[0]], seq_buf, sems.at[0])
    copies = []
    for h in range(4):
        row = pl.multiple_of((col // 4 * 4 + h) * HEAD, HEAD)
        copies.append(pltpu.make_async_copy(near_hbm.at[pl.ds(h * n, n)], all_buf.at[h], sems.at[1 + 5 * h]))
        for k, window in enumerate(windows):
            weight = w_hbm.at[pl.ds(row, HEAD), window]
            low = wl_buf.at[pl.ds(h * 256, HEAD), pl.ds(256 * k, 256)]
            high = wh_buf.at[pl.ds(h * 256 + 64, HEAD), pl.ds(256 * k, 256)]
            copies.append(pltpu.make_async_copy(weight, low, sems.at[2 + 5 * h + 2 * k]))
            copies.append(pltpu.make_async_copy(weight, high, sems.at[3 + 5 * h + 2 * k]))
    for copy in copies:
        copy.start()
    seq_copy.start()
    for h in range(4):
        wl_buf[h * 256 + HEAD : (h + 1) * 256, :] = jnp.zeros((64, 512), bf16)
        wh_buf[h * 256 : h * 256 + 64, :] = jnp.zeros((64, 512), bf16)
    for copy in copies:
        copy.wait()
    seq_copy.wait()
    for side, w_buf in ((0, wl_buf), (1, wh_buf)):
        lhs = jnp.concatenate([all_buf[h][:, 128 * side : 128 * side + 256] for h in range(4)], axis=1)
        part = jnp.dot(lhs, w_buf[...], preferred_element_type=f32)
        at = slice(side * n, (side + 1) * n)
        turned[:256, at] = (part[:, :256] + seq_buf[at, :].astype(f32)).T
        turned[256:, at] = part[:, 256:].T
    offset = pl.multiple_of(lax.rem(col, 2) * 64, 64)
    mine_ref[...] = turned[pl.ds(offset, HEAD), :]
    sent_ref[...] = turned[pl.ds(pl.multiple_of(256 + offset, 64), HEAD), :].astype(bf16)


def trunk_parts(place, near, sequence, out_weight):
    vmem = pl.BlockSpec(memory_space=pltpu.VMEM)
    hbm = pl.BlockSpec(memory_space=pl.ANY)
    rows = sequence.shape[0]
    return pl.pallas_call(
        trunk_kernel,
        in_specs=[pl.BlockSpec(memory_space=pltpu.SMEM)] + [hbm] * 3,
        out_specs=[vmem] * 2,
        out_shape=[jax.ShapeDtypeStruct((HEAD, rows), f32), jax.ShapeDtypeStruct((HEAD, rows), bf16)],
        scratch_shapes=[
            pltpu.VMEM((4, rows // 2, 2 * HEAD), bf16),
            pltpu.VMEM((rows, 256), bf16),
            pltpu.VMEM((4 * 256, 512), bf16),
            pltpu.VMEM((4 * 256, 512), bf16),
            pltpu.VMEM((512, rows), f32),
            pltpu.SemaphoreType.DMA((21,)),
        ],
        compiler_params=params(),
        name="trunk_parts",
        cost_estimate=pl.CostEstimate(flops=1_100_000_000, bytes_accessed=5_000_000, transcendentals=0),
    )(place, near, sequence, out_weight)


def add_kernel(mine_ref, got_ref, order_ref, out_ref):
    out_ref[...] = (mine_ref[...] + got_ref[...].astype(f32)).astype(bf16)


def add_parts(mine, got, order):
    vmem = pl.BlockSpec(memory_space=pltpu.VMEM)
    return pl.pallas_call(
        add_kernel,
        in_specs=[vmem, vmem, pl.BlockSpec(memory_space=pl.ANY)],
        out_specs=vmem,
        out_shape=jax.ShapeDtypeStruct(mine.shape, bf16),
        compiler_params=params(8 * 2**20),
        name="add_parts",
    )(mine, got, order)


def per_device(
    sequence,
    norm_gain,
    query_weight,
    key_weight,
    value_weight,
    out_weight,
    pool_gain,
    row_weight,
    column_weight,
    conv_near,
    conv_far,
    trans_gain,
    trans_in,
    trans_out,
):
    place = jnp.stack([lax.axis_index("ctx"), lax.axis_index("col")]).astype(jnp.int32)
    spots = range(16)
    cols = range(8)
    to_core = [(i, i ^ 1) for i in spots]
    to_z = [(i, i ^ 8) for i in spots]
    to_up = [(i, (i & 8) | ((i + 2) & 7)) for i in spots]
    to_down = [(i, (i & 8) | ((i - 2) & 7)) for i in spots]

    def send(x, perm):
        return lax.ppermute(x, "ctx", perm)

    kv, query, mean_low, mean_high = project(sequence, norm_gain, query_weight, key_weight, value_weight)
    kv_core = send(kv, to_core)
    query_z = send(query, to_z)
    kv_below = send(kv, to_up)
    kv_above = send(kv, to_down)
    state = attend(query, [kv, kv_core])
    gain_row = pool_gain.reshape(1, -1)
    trans_row = trans_gain.reshape(1, -1)
    state_z = attend(query_z, [kv, kv_core], orders=(gain_row, trans_row, place))
    low, high = cut(kv_below, kv_above, state, state_z)
    far_below = send(low, to_up)
    far_above = send(high, to_down)
    twin = [send(kv_below, to_core), send(kv_above, to_core)]
    state_z = attend(query_z, [kv_below, kv_above], state_z)
    opposite = join(far_below, far_above, state_z)
    opposite_core = send(opposite, to_core)
    state_z = attend(query_z, twin, state_z)
    returned = attend(query_z, [opposite, opposite_core], state_z, mode="remote")
    other = send(returned, to_z)
    rest = [kv_below, kv_above, *twin, opposite, opposite_core]
    mine, log = attend(query, rest, state, mode="final")
    attended, pool = merge(mine, log, other)

    along_y = [[0, 1, 2, 3], [4, 5, 6, 7]]
    near_heads = lax.all_gather(attended, "col", axis=0, tiled=True, axis_index_groups=along_y)
    pools = lax.all_to_all(pool, "col", 0, 0)
    row, sent = features(
        pools, mean_low, mean_high, out_weight, gain_row, row_weight, column_weight, lax.axis_size("ctx")
    )
    got = lax.all_to_all(sent, "ctx", 0, 0)
    mine_cols, sent_cols = trunk_parts(place, near_heads, sequence, out_weight)
    got_cols = lax.ppermute(sent_cols, "col", [(i, i ^ 4) for i in cols])
    pair_out = pair_map(
        place, row, got, conv_near, conv_far, trans_row, trans_in, trans_out, sent_cols
    )
    trunk_out = add_parts(mine_cols, got_cols, pair_out).T
    return (trunk_out, pair_out)


def solution(mesh):
    return jax.shard_map(
        per_device,
        mesh=mesh,
        in_specs=(
            P("ctx", None),
            P(),
            P(None, "col"),
            P(None, "col"),
            P(None, "col"),
            P(),
            P(),
            P(),
            P(),
            P(),
            P(),
            P(),
            P(),
            P(),
        ),
        out_specs=(P("ctx", "col"), P("ctx", "col", None)),
        check_vma=False,
    )
```

```python
import functools
import math

import jax
import jax.numpy as jnp
from jax import lax
from jax.experimental import pallas as pl
from jax.experimental.pallas import tpu as pltpu
from jax.sharding import PartitionSpec as P

POOL = 16
HEAD = 192
EPSILON = 1e-06
LAYER_EPSILON = 1e-05
OUTSIDE = -1e30
SCALE = math.log2(math.e) / math.sqrt(HEAD)
bf16 = jnp.bfloat16
f32 = jnp.float32
VMEM = 56 * 2**20


def params(limit=VMEM):
    return pltpu.CompilerParams(vmem_limit_bytes=limit)


def lanes_of(shape):
    return lax.broadcasted_iota(jnp.int32, shape, len(shape) - 1)


def pack_lanes(low, high):
    rolled = pltpu.roll(high, 64, axis=1)
    middle = jnp.where(lanes_of(rolled.shape) < 64, pltpu.roll(low, 128, axis=1), rolled)
    return jnp.concatenate([low[:, :128], middle], axis=1)


def unpack_query(packed):
    wide = pltpu.roll(packed[:, :256].astype(f32), 64, axis=1)
    lane = lanes_of(wide.shape)
    low = jnp.where(lane < 64, 0.0, wide).astype(bf16)
    high = jnp.where(lane < 64, 0.0, packed[:, 128:].astype(f32)).astype(bf16)
    return jnp.concatenate([low, high], axis=0)


def normalised(x, gain):
    square = jnp.mean(x * x, axis=-1, keepdims=True)
    return (x * lax.rsqrt(square + EPSILON) * gain).astype(bf16)


def turned_dot(a, b):
    return lax.dot_general(a, b, (((1,), (1,)), ((), ())), preferred_element_type=f32)


def project_kv_kernel(seq_ref, gain_ref, wk_ref, wv_ref, kv_ref):
    gain = gain_ref[...].astype(f32).reshape(1, -1)
    weights = jnp.concatenate([wv_ref[...], wk_ref[...]], axis=0)
    rows = seq_ref.shape[0]
    part = rows // 2
    for start in range(0, rows, part):
        normed = normalised(seq_ref[start : start + part, :].astype(f32), gain)
        kv_ref[start : start + part, :] = turned_dot(normed, weights).astype(bf16)


def project_kv(sequence, gain, wk, wv):
    rows, feat = sequence.shape
    steps = 2
    whole = lambda a: pl.BlockSpec(a.shape, lambda t: (0,) * a.ndim)
    wk, wv = wk.T, wv.T
    return pl.pallas_call(
        project_kv_kernel,
        grid=(steps,),
        in_specs=[pl.BlockSpec((rows // steps, feat), lambda t: (t, 0)), whole(gain), whole(wk), whole(wv)],
        out_specs=pl.BlockSpec((rows // steps, 2 * HEAD), lambda t: (t, 0)),
        out_shape=jax.ShapeDtypeStruct((rows, 2 * HEAD), bf16),
        compiler_params=params(),
        name="project_kv",
        cost_estimate=pl.CostEstimate(flops=4 * rows * feat * HEAD, bytes_accessed=5_000_000, transcendentals=0),
    )(sequence, gain, wk, wv)


def project_q_kernel(low_ref, high_ref, gain_ref, wq_ref, q_ref, ml_ref, mh_ref):
    gain = gain_ref[...].astype(f32).reshape(1, -1)
    rows = low_ref.shape[0]
    part = rows // 2
    for start in range(0, rows, part):
        halves = []
        for ref, mean_ref in ((low_ref, ml_ref), (high_ref, mh_ref)):
            x = ref[start : start + part, :].astype(f32)
            mean = jnp.mean(x.reshape(part // POOL, POOL, x.shape[1]), axis=1)
            mean_ref[start // POOL : (start + part) // POOL, :] = mean
            halves.append(normalised(x, gain))
        q = turned_dot(jnp.concatenate(halves, axis=0), wq_ref[...]) * SCALE
        q = jnp.concatenate([q, jnp.zeros((2 * part, 64), f32)], axis=1)
        q_ref[start : start + part, :] = pack_lanes(q[:part], q[part:]).astype(bf16)


def project_q(sequence, gain, wq):
    rows, feat = sequence.shape
    steps = 2
    tile = rows // 2 // steps
    whole = lambda a: pl.BlockSpec(a.shape, lambda t: (0,) * a.ndim)
    wq = wq.T
    return pl.pallas_call(
        project_q_kernel,
        grid=(steps,),
        in_specs=[
            pl.BlockSpec((tile, feat), lambda t: (t, 0)),
            pl.BlockSpec((tile, feat), lambda t: (t + steps, 0)),
            whole(gain),
            whole(wq),
        ],
        out_specs=[
            pl.BlockSpec((tile, 2 * HEAD), lambda t: (t, 0)),
            pl.BlockSpec((tile // POOL, feat), lambda t: (t, 0)),
            pl.BlockSpec((tile // POOL, feat), lambda t: (t, 0)),
        ],
        out_shape=[
            jax.ShapeDtypeStruct((rows // 2, 2 * HEAD), bf16),
            jax.ShapeDtypeStruct((rows // 2 // POOL, feat), f32),
            jax.ShapeDtypeStruct((rows // 2 // POOL, feat), f32),
        ],
        compiler_params=params(),
        name="project_q",
        cost_estimate=pl.CostEstimate(flops=2 * rows * feat * HEAD, bytes_accessed=5_000_000, transcendentals=0),
    )(sequence, sequence, gain, wq)


SUB = 256
CHUNK = 1024


def log_rows(logs):
    rows = []
    for log in logs:
        for g in range(log.shape[0] // 128):
            block = jnp.broadcast_to(log[g * 128 : (g + 1) * 128], (128, 128))
            rows.append(block.T[:1])
    return jnp.concatenate(rows, axis=0)


def attend_kernel(*refs, sizes, carried, mode, orders):
    count = len(sizes)
    q_hbm = refs[0]
    kv_hbm = refs[1 : 1 + count]
    rest = list(refs[1 + count :])
    state_hbm = rest.pop(0) if carried else None
    rest = rest[orders:]
    out_hbm = rest.pop(0)
    log_hbm = rest.pop(0) if mode == "final" else None
    q_buf, kv_buf, v_buf, state_buf, out_buf, log_buf, sems = rest
    q_copy = pltpu.make_async_copy(q_hbm, q_buf, sems.at[0])
    q_copy.start()
    copies = []
    at = 0
    for n, (ref, size) in enumerate(zip(kv_hbm, sizes)):
        copy = pltpu.make_async_copy(ref, kv_buf.at[pl.ds(at, size)], sems.at[7 + n])
        copy.start()
        copies.append((at, size, copy))
        at += size
    keys = at
    if carried:
        state_copy = pltpu.make_async_copy(state_hbm, state_buf, sems.at[1])
        state_copy.start()
    q_copy.wait()
    queries = unpack_query(q_buf[...])
    subs = queries.shape[0] // SUB
    chunks = keys // CHUNK
    half = subs // 2
    order = range(subs) if mode == "state" else [i + s * half for i in range(half) for s in range(2)]
    units = [(i, c) for i in order for c in range(chunks)]
    out_copies = []

    def store(rows):
        part = pl.ds(rows[0], rows[1])
        copy = pltpu.make_async_copy(out_buf.at[part], out_hbm.at[part], sems.at[2 + len(out_copies)])
        copy.start()
        out_copies.append(copy)

    def score(unit):
        i, c = unit
        if i == 0:
            for at, size, copy in copies:
                if c * CHUNK <= at < (c + 1) * CHUNK:
                    copy.wait()
            v = kv_buf[c * CHUNK : (c + 1) * CHUNK, :256]
            lane = lanes_of(v.shape)
            v_buf[c * CHUNK : (c + 1) * CHUNK, :] = jnp.where(
                lane < HEAD, v, jnp.where(lane == HEAD, 1.0, 0.0).astype(bf16)
            )
        return lax.dot_general(
            queries[i * SUB : (i + 1) * SUB],
            kv_buf[c * CHUNK : (c + 1) * CHUNK, 128:],
            (((1,), (1,)), ((), ())),
            preferred_element_type=f32,
        )

    following = score(units[0])
    results = {}
    top = total = None
    for n, (i, c) in enumerate(units):
        scores = following
        if n + 1 < len(units):
            following = score(units[n + 1])
        here = jnp.max(scores, axis=1, keepdims=True)
        new = here if c == 0 else jnp.maximum(top, here)
        weights = jnp.exp2(scores - new).astype(bf16)
        mixed = jnp.dot(weights, v_buf[c * CHUNK : (c + 1) * CHUNK, :], preferred_element_type=f32)
        total = mixed if c == 0 else total * jnp.exp2(top - new) + mixed
        top = new
        if c < chunks - 1:
            continue
        if carried:
            if i == 0:
                state_copy.wait()
            before = state_buf[i * SUB : (i + 1) * SUB, :]
            old = before[:, HEAD + 1 : HEAD + 2]
            new = jnp.maximum(top, old)
            total = total * jnp.exp2(top - new) + before * jnp.exp2(old - new)
            top = new
        if mode == "state":
            out_buf[i * SUB : (i + 1) * SUB, :] = jnp.where(lanes_of(total.shape) == HEAD + 1, top, total)
            store((i * SUB, SUB))
            continue
        sums = total[:, HEAD : HEAD + 1]
        results[i] = (total * (1.0 / sums), top + jnp.log2(sums))
        if i >= half:
            packed = pack_lanes(results[i - half][0], results[i][0])
            out_buf[(i - half) * SUB : (i - half + 1) * SUB, :] = packed.astype(out_buf.dtype)
            store(((i - half) * SUB, SUB))
    if mode != "state":
        rows = log_rows([results[i][1] for i in range(subs)])
    if mode == "remote":
        rows = jnp.concatenate([rows, jnp.zeros((16 - rows.shape[0], 128), f32)], axis=0)
        first = rows.astype(bf16)
        left = rows - first.astype(f32)
        second = left.astype(bf16)
        third = (left - second.astype(f32)).astype(bf16)
        out_buf[half * SUB :, :] = jnp.concatenate([first, second, third], axis=1)
        store((half * SUB, 16))
    if mode == "final":
        log_buf[...] = rows
        copy = pltpu.make_async_copy(log_buf, log_hbm, sems.at[6])
        copy.start()
        out_copies.append(copy)
    for copy in out_copies:
        copy.wait()


def attend(query, kvs, state=None, mode="state", orders=()):
    rows = query.shape[0]
    sizes = tuple(kv.shape[0] for kv in kvs)
    keys = sum(sizes)
    args = [query, *kvs] + ([] if state is None else [state]) + list(orders)
    out_shape = {
        "state": [jax.ShapeDtypeStruct((2 * rows, 256), f32)],
        "remote": [jax.ShapeDtypeStruct((rows + 16, 2 * HEAD), bf16)],
        "final": [
            jax.ShapeDtypeStruct((rows, 2 * HEAD), f32),
            jax.ShapeDtypeStruct((2 * rows // 128, 128), f32),
        ],
    }[mode]
    hbm = pl.BlockSpec(memory_space=pl.ANY)
    out = pl.pallas_call(
        functools.partial(attend_kernel, sizes=sizes, carried=state is not None, mode=mode, orders=len(orders)),
        in_specs=[hbm] * len(args),
        out_specs=[hbm] * len(out_shape),
        out_shape=out_shape,
        scratch_shapes=[
            pltpu.VMEM(query.shape, bf16),
            pltpu.VMEM((keys, 2 * HEAD), bf16),
            pltpu.VMEM((keys, 256), bf16),
            pltpu.VMEM((2 * rows if state is not None else 8, 256), f32),
            pltpu.VMEM(out_shape[0].shape, out_shape[0].dtype),
            pltpu.VMEM((8, 128), f32),
            pltpu.SemaphoreType.DMA((7 + len(kvs),)),
        ],
        compiler_params=params(36 * 2**20),
        name="attend_" + mode,
        cost_estimate=pl.CostEstimate(
            flops=2 * 2 * rows * keys * 512, bytes_accessed=4_000_000, transcendentals=2 * rows * keys
        ),
    )(*args)
    return out if mode == "final" else out[0]


def cut_kernel(below_ref, above_ref, *refs):
    out_low_ref, out_high_ref, sems = refs[-3:]
    n = out_low_ref.shape[0]
    low = pltpu.make_async_copy(below_ref.at[pl.ds(0, n)], out_low_ref, sems.at[0])
    high = pltpu.make_async_copy(above_ref.at[pl.ds(n, n)], out_high_ref, sems.at[1])
    low.start()
    high.start()
    low.wait()
    high.wait()


def cut(below, above, *orders):
    hbm = pl.BlockSpec(memory_space=pl.ANY)
    part = jax.ShapeDtypeStruct((below.shape[0] // 2, below.shape[1]), below.dtype)
    return pl.pallas_call(
        cut_kernel,
        in_specs=[hbm] * (2 + len(orders)),
        out_specs=[hbm] * 2,
        out_shape=[part] * 2,
        scratch_shapes=[pltpu.SemaphoreType.DMA((2,))],
        compiler_params=params(2**20),
        name="cut",
    )(below, above, *orders)


def join_kernel(low_ref, high_ref, order_ref, out_ref, sems):
    n = low_ref.shape[0]
    low = pltpu.make_async_copy(low_ref, out_ref.at[pl.ds(0, n)], sems.at[0])
    high = pltpu.make_async_copy(high_ref, out_ref.at[pl.ds(n, n)], sems.at[1])
    low.start()
    high.start()
    low.wait()
    high.wait()


def join(low, high, order):
    hbm = pl.BlockSpec(memory_space=pl.ANY)
    return pl.pallas_call(
        join_kernel,
        in_specs=[hbm] * 3,
        out_specs=hbm,
        out_shape=jax.ShapeDtypeStruct((2 * low.shape[0], low.shape[1]), low.dtype),
        scratch_shapes=[pltpu.SemaphoreType.DMA((2,))],
        compiler_params=params(2**20),
        name="join",
    )(low, high, order)


def relay_kernel(x_ref, *refs):
    out_ref, sem = refs[-2:]
    copy = pltpu.make_async_copy(x_ref, out_ref, sem)
    copy.start()
    copy.wait()


def relay(x, *orders):
    hbm = pl.BlockSpec(memory_space=pl.ANY)
    return pl.pallas_call(
        relay_kernel,
        in_specs=[hbm] * (1 + len(orders)),
        out_specs=hbm,
        out_shape=jax.ShapeDtypeStruct(x.shape, x.dtype),
        scratch_shapes=[pltpu.SemaphoreType.DMA],
        compiler_params=params(2**20),
        name="relay",
    )(x, *orders)


def merge_kernel(mine_ref, log_ref, other_ref, out_ref, pool_ref):
    n = out_ref.shape[0]
    stats = other_ref[n:, :].astype(f32)
    rows = (stats[:, :128] + stats[:, 128:256] + stats[:, 256:])[: 2 * n // 128]
    share = 1.0 / (1.0 + jnp.exp2(log_ref[...] - rows))
    columns = []
    for g in range(2 * n // 128):
        columns.append(jnp.broadcast_to(share[g : g + 1], (128, 128)).T)
    low = jnp.concatenate(columns[: n // 128], axis=0)
    high = jnp.concatenate(columns[n // 128 :], axis=0)
    middle = jnp.where(lanes_of(low.shape) < 64, low, high)
    share = jnp.concatenate([low, middle, high], axis=1)
    mine = mine_ref[...]
    attended = (mine + share * (other_ref[:n, :].astype(f32) - mine)).astype(bf16)
    out_ref[...] = attended
    wide = attended.astype(f32)
    pool = jnp.mean(wide.reshape(n // POOL, POOL, wide.shape[1]), axis=1).astype(bf16)
    for k in range(pool_ref.shape[0]):
        pool_ref[k] = pool


def merge(mine, log, other):
    rows = mine.shape[0]
    vmem = pl.BlockSpec(memory_space=pltpu.VMEM)
    return pl.pallas_call(
        merge_kernel,
        in_specs=[vmem] * 3,
        out_specs=[vmem] * 2,
        out_shape=[
            jax.ShapeDtypeStruct((rows, 2 * HEAD), bf16),
            jax.ShapeDtypeStruct((8, rows // POOL, 2 * HEAD), bf16),
        ],
        compiler_params=params(16 * 2**20),
        name="merge",
    )(mine, log, other)


def features_kernel(*refs):
    sources, rest = refs[:7], refs[7:]
    rout_ref, sent_ref, pool_ref, ml_ref, mh_ref, w_ref, gain_ref, row_ref, col_ref, sems = rest
    held = (pool_ref, ml_ref, mh_ref, w_ref, gain_ref, row_ref, col_ref)
    parts = 6
    depth = w_ref.shape[0] // parts
    copies = {}
    for n in (0, 3, 1, 2, 4, 5, 6):
        if n == 3:
            w_copies = []
            for p in range(parts):
                piece = pl.ds(p * depth, depth)
                w_copies.append(pltpu.make_async_copy(sources[3].at[piece], w_ref.at[piece], sems.at[p]))
                w_copies[p].start()
        else:
            copies[n] = pltpu.make_async_copy(sources[n], held[n], sems.at[parts + n])
            copies[n].start()
    copies[0].wait()
    heads = []
    for h in range(8):
        packed = pool_ref[h].astype(f32)
        low, high = packed[:, :256], pltpu.roll(packed[:, 128:], 192, axis=1)
        heads.append(jnp.concatenate([low, high], axis=0)[:, :HEAD])
    lhs = jnp.concatenate(heads, axis=1).astype(bf16)
    pooled = None
    for p in range(parts):
        w_copies[p].wait()
        piece = slice(p * depth, (p + 1) * depth)
        product = jnp.dot(lhs[:, piece], w_ref[piece, :], preferred_element_type=f32)
        pooled = product if pooled is None else pooled + product
    for n in (1, 2, 4, 5, 6):
        copies[n].wait()
    pooled = pooled + jnp.concatenate([ml_ref[...], mh_ref[...]], axis=0)
    inverse = lax.rsqrt(jnp.mean(pooled * pooled, axis=-1, keepdims=True) + EPSILON)
    scaled = (pooled * gain_ref[...].astype(f32)).astype(bf16)
    weights = jnp.concatenate([row_ref[...], col_ref[...]], axis=1)
    got = (inverse * jnp.dot(scaled, weights, preferred_element_type=f32)).astype(bf16).astype(f32)
    channels = rout_ref.shape[1]
    row, col = got[:, :channels], got[:, channels:]
    rout_ref[...] = row.astype(bf16)
    sent = jnp.concatenate([col, row[:8], row[-8:]], axis=0).astype(bf16)
    for k in range(sent_ref.shape[0]):
        sent_ref[k] = sent


def features(pools, mean_low, mean_high, out_weight, gain, row_weight, column_weight, copies):
    rows = 2 * mean_low.shape[0]
    channels = row_weight.shape[1]
    vmem = pl.BlockSpec(memory_space=pltpu.VMEM)
    hbm = pl.BlockSpec(memory_space=pl.ANY)
    return pl.pallas_call(
        features_kernel,
        in_specs=[hbm] * 7,
        out_specs=[vmem] * 2,
        out_shape=[
            jax.ShapeDtypeStruct((rows, channels), bf16),
            jax.ShapeDtypeStruct((copies, rows + 16, channels), bf16),
        ],
        scratch_shapes=[
            pltpu.VMEM(a.shape, a.dtype)
            for a in (pools, mean_low, mean_high, out_weight, gain, row_weight, column_weight)
        ]
        + [pltpu.SemaphoreType.DMA((13,))],
        compiler_params=params(),
        name="features",
    )(pools, mean_low, mean_high, out_weight, gain, row_weight, column_weight)


def pair_kernel(
    place_ref, row_ref, got_ref, near_ref, far_ref, gain_ref, in_ref, tout_ref, order_ref,
    out_ref, row_buf, col_buf, wn_ref, wf_ref, xn_ref, xf_ref, first_ref, second_ref,
):
    rows, cols, channels = out_ref.shape
    ctx, col = place_ref[0], place_ref[1]
    gone = jnp.full((8, channels), OUTSIDE, f32)
    spots = got_ref.shape[0]
    above = got_ref[jnp.maximum(ctx - 1, 0)][rows + 8 :].astype(f32)
    below = got_ref[jnp.minimum(ctx + 1, spots - 1)][rows : rows + 8].astype(f32)
    row_buf[:8] = jnp.where(ctx == 0, gone, above)
    row_buf[8 : 8 + rows] = row_ref[...].astype(f32)
    row_buf[8 + rows :] = jnp.where(ctx == spots - 1, gone, below)
    half = cols // 2
    left = got_ref[jnp.maximum(2 * col - 1, 0)][half - 8 : half].astype(f32)
    right = got_ref[jnp.minimum(2 * col + 2, spots - 1)][:8].astype(f32)
    col_buf[:8] = jnp.where(col == 0, gone, left)
    col_buf[8 : 8 + half] = got_ref[2 * col][:half].astype(f32)
    col_buf[8 + half : 8 + cols] = got_ref[2 * col + 1][:half].astype(f32)
    col_buf[8 + cols :] = jnp.where(2 * col + 2 >= spots, gone, right)

    blank = jnp.zeros((channels, channels), bf16)
    for kernel_ref, w_ref in ((near_ref, wn_ref), (far_ref, wf_ref)):
        for a in range(4):
            for b in range(3):
                at = (a * 3 + b) * channels
                w_ref[at : at + channels, :channels] = kernel_ref[a, b] if a < 3 else blank
                w_ref[at : at + channels, channels:] = kernel_ref[a - 1, b] if a > 0 else blank

    span = cols + 8
    shifted = [col_buf[2 + 2 * b : 2 + 2 * b + span, :] for b in range(3)]
    taps = jnp.concatenate(shifted, axis=1)

    def fill(r):
        row = row_buf[pl.ds(r + 2, 1), :]
        triple = jnp.concatenate([row, row, row], axis=1)
        xn_ref[r] = jnp.maximum(triple + taps, 0.0).astype(bf16)

    def near_step(g):
        start = g * 8
        lhs = []
        for k in (0, 1, 4, 5):
            lhs.append(jnp.concatenate([xn_ref[start + k + 2 * a] for a in range(4)], axis=1))
        got = jnp.dot(jnp.concatenate(lhs, axis=0), wn_ref[...], preferred_element_type=f32)
        for n, k in enumerate((0, 1, 4, 5)):
            for side in range(2):
                r = start + k + 2 * side
                part = got[n * span : (n + 1) * span, side * channels : (side + 1) * channels]
                first = part + row_buf[pl.ds(r + 4, 1), :] + shifted[1]
                centre = first[4 : 4 + cols]
                first_ref[r] = centre
                hidden = jnp.concatenate([first[:cols], centre, first[8 : 8 + cols]], axis=1)
                xf_ref[r] = jnp.maximum(hidden, 0.0).astype(bf16)

    def far_step(g):
        start = g * 8
        lhs = []
        for k in range(4):
            lhs.append(jnp.concatenate([xf_ref[start + k + 4 * a] for a in range(4)], axis=1))
        got = jnp.dot(jnp.concatenate(lhs, axis=0), wf_ref[...], preferred_element_type=f32)
        for side in range(2):
            for k in range(4):
                part = got[k * cols : (k + 1) * cols, side * channels : (side + 1) * channels]
                second_ref[4 * side + k] = part + first_ref[start + 4 * side + k + 4]

    def transition_step(g):
        start = g * 8
        second = second_ref[...].reshape(8 * cols, channels)
        centred = second - jnp.mean(second, axis=-1, keepdims=True)
        variance = jnp.mean(centred * centred, axis=-1, keepdims=True)
        layer = (centred * lax.rsqrt(variance + LAYER_EPSILON) * gain_ref[...].astype(f32)).astype(bf16)
        middle = jnp.dot(layer, in_ref[...], preferred_element_type=f32)
        middle = jnp.maximum(middle, 0.0).astype(bf16)
        result = (second + jnp.dot(middle, tout_ref[...], preferred_element_type=f32)).astype(bf16)
        for k in range(8):
            out_ref[start + k] = result[k * cols : (k + 1) * cols]

    last = rows // 8
    for r in range(12):
        fill(r)

    def fill_for(g):
        for r in range(8):
            fill(g * 8 + 4 + r)

    near_step(0)
    fill_for(1)
    near_step(1)
    fill_for(2)
    far_step(0)
    near_step(2)
    fill_for(3)

    def steady(g, carry):
        near_step(g)
        transition_step(g - 3)
        far_step(g - 2)

        @pl.when(g < last)
        def _():
            fill_for(g + 1)

        return carry

    lax.fori_loop(3, last + 1, steady, 0)
    transition_step(last - 2)
    far_step(last - 1)
    transition_step(last - 1)


def pair_map(place, row, got, near, far, gain, trans_in, trans_out, order):
    rows, channels = row.shape
    cols = 2 * rows
    vmem = pl.BlockSpec(memory_space=pltpu.VMEM)
    return pl.pallas_call(
        pair_kernel,
        in_specs=[pl.BlockSpec(memory_space=pltpu.SMEM)] + [vmem] * 7 + [pl.BlockSpec(memory_space=pl.ANY)],
        out_specs=vmem,
        out_shape=jax.ShapeDtypeStruct((rows, cols, channels), bf16),
        scratch_shapes=[
            pltpu.VMEM((rows + 16, channels), f32),
            pltpu.VMEM((cols + 16, channels), f32),
            pltpu.VMEM((12 * channels, 2 * channels), bf16),
            pltpu.VMEM((12 * channels, 2 * channels), bf16),
            pltpu.VMEM((rows + 12, cols + 8, 3 * channels), bf16),
            pltpu.VMEM((rows + 8, cols, 3 * channels), bf16),
            pltpu.VMEM((rows + 8, cols, channels), f32),
            pltpu.VMEM((8, cols, channels), f32),
        ],
        compiler_params=params(),
        name="pair_map",
        cost_estimate=pl.CostEstimate(flops=14_000_000_000, bytes_accessed=3_000_000, transcendentals=0),
    )(place, row, got, near, far, gain, trans_in, trans_out, order)


def trunk_kernel(place_ref, near_hbm, seq_hbm, w_hbm, mine_ref, sent_ref, all_buf, seq_buf, wl_buf, wh_buf, turned, sems):
    n = all_buf.shape[1]
    col = place_ref[1]
    other = lax.rem(col + 4, 8)
    windows = [pl.ds(pl.multiple_of((c * 3 // 2) * 128, 128), 256) for c in (col, other)]
    seq_copy = pltpu.make_async_copy(seq_hbm.at[:, windows[0]], seq_buf, sems.at[0])
    copies = []
    for h in range(4):
        row = pl.multiple_of((col // 4 * 4 + h) * HEAD, HEAD)
        copies.append(pltpu.make_async_copy(near_hbm.at[pl.ds(h * n, n)], all_buf.at[h], sems.at[1 + 5 * h]))
        for k, window in enumerate(windows):
            weight = w_hbm.at[pl.ds(row, HEAD), window]
            low = wl_buf.at[pl.ds(h * 256, HEAD), pl.ds(256 * k, 256)]
            high = wh_buf.at[pl.ds(h * 256 + 64, HEAD), pl.ds(256 * k, 256)]
            copies.append(pltpu.make_async_copy(weight, low, sems.at[2 + 5 * h + 2 * k]))
            copies.append(pltpu.make_async_copy(weight, high, sems.at[3 + 5 * h + 2 * k]))
    for copy in copies:
        copy.start()
    seq_copy.start()
    for h in range(4):
        wl_buf[h * 256 + HEAD : (h + 1) * 256, :] = jnp.zeros((64, 512), bf16)
        wh_buf[h * 256 : h * 256 + 64, :] = jnp.zeros((64, 512), bf16)
    for copy in copies:
        copy.wait()
    seq_copy.wait()
    for side, w_buf in ((0, wl_buf), (1, wh_buf)):
        lhs = jnp.concatenate([all_buf[h][:, 128 * side : 128 * side + 256] for h in range(4)], axis=1)
        part = jnp.dot(lhs, w_buf[...], preferred_element_type=f32)
        at = slice(side * n, (side + 1) * n)
        turned[:256, at] = (part[:, :256] + seq_buf[at, :].astype(f32)).T
        turned[256:, at] = part[:, 256:].T
    offset = pl.multiple_of(lax.rem(col, 2) * 64, 64)
    mine_ref[...] = turned[pl.ds(offset, HEAD), :]
    sent_ref[...] = turned[pl.ds(pl.multiple_of(256 + offset, 64), HEAD), :].astype(bf16)


def trunk_parts(place, near, sequence, out_weight):
    vmem = pl.BlockSpec(memory_space=pltpu.VMEM)
    hbm = pl.BlockSpec(memory_space=pl.ANY)
    rows = sequence.shape[0]
    return pl.pallas_call(
        trunk_kernel,
        in_specs=[pl.BlockSpec(memory_space=pltpu.SMEM)] + [hbm] * 3,
        out_specs=[vmem] * 2,
        out_shape=[jax.ShapeDtypeStruct((HEAD, rows), f32), jax.ShapeDtypeStruct((HEAD, rows), bf16)],
        scratch_shapes=[
            pltpu.VMEM((4, rows // 2, 2 * HEAD), bf16),
            pltpu.VMEM((rows, 256), bf16),
            pltpu.VMEM((4 * 256, 512), bf16),
            pltpu.VMEM((4 * 256, 512), bf16),
            pltpu.VMEM((512, rows), f32),
            pltpu.SemaphoreType.DMA((21,)),
        ],
        compiler_params=params(),
        name="trunk_parts",
        cost_estimate=pl.CostEstimate(flops=1_100_000_000, bytes_accessed=5_000_000, transcendentals=0),
    )(place, near, sequence, out_weight)


def add_kernel(mine_ref, got_ref, order_ref, out_ref):
    out_ref[...] = (mine_ref[...] + got_ref[...].astype(f32)).astype(bf16)


def add_parts(mine, got, order):
    vmem = pl.BlockSpec(memory_space=pltpu.VMEM)
    return pl.pallas_call(
        add_kernel,
        in_specs=[vmem, vmem, pl.BlockSpec(memory_space=pl.ANY)],
        out_specs=vmem,
        out_shape=jax.ShapeDtypeStruct(mine.shape, bf16),
        compiler_params=params(8 * 2**20),
        name="add_parts",
    )(mine, got, order)


def per_device(
    sequence,
    norm_gain,
    query_weight,
    key_weight,
    value_weight,
    out_weight,
    pool_gain,
    row_weight,
    column_weight,
    conv_near,
    conv_far,
    trans_gain,
    trans_in,
    trans_out,
):
    place = jnp.stack([lax.axis_index("ctx"), lax.axis_index("col")]).astype(jnp.int32)
    spots = range(16)
    cols = range(8)
    to_core = [(i, i ^ 1) for i in spots]
    to_z = [(i, i ^ 8) for i in spots]
    to_up = [(i, (i & 8) | ((i + 2) & 7)) for i in spots]
    to_down = [(i, (i & 8) | ((i - 2) & 7)) for i in spots]

    def send(x, perm):
        return lax.ppermute(x, "ctx", perm)

    kv = project_kv(sequence, norm_gain, key_weight, value_weight)
    kv_core = send(kv, to_core)
    kv_below = send(kv, to_up)
    kv_above = send(kv, to_down)
    query, mean_low, mean_high = project_q(sequence, norm_gain, query_weight)
    query_z = send(query, to_z)
    state = attend(query, [kv, kv_core])
    gain_row = pool_gain.reshape(1, -1)
    trans_row = trans_gain.reshape(1, -1)
    low, high = cut(kv_below, kv_above, state)
    far_below = send(low, to_up)
    far_above = send(high, to_down)
    twin = [send(kv_below, to_core), send(kv_above, to_core)]
    state_z = attend(query_z, [kv, kv_core, kv_below, kv_above], orders=(low, gain_row, trans_row, place))
    opposite = join(far_below, far_above, state_z)
    opposite_core = send(opposite, to_core)
    state_z = attend(query_z, twin, state_z)
    returned = attend(query_z, [opposite, opposite_core], state_z, mode="remote")
    other = send(returned, to_z)
    rest = [kv_below, kv_above, *twin, opposite, opposite_core]
    mine, log = attend(query, rest, state, mode="final")
    attended, pool = merge(mine, log, other)

    along_y = [[0, 1, 2, 3], [4, 5, 6, 7]]
    near_heads = lax.all_gather(attended, "col", axis=0, tiled=True, axis_index_groups=along_y)
    pools = lax.all_to_all(pool, "col", 0, 0)
    row, sent = features(
        pools, mean_low, mean_high, out_weight, gain_row, row_weight, column_weight, lax.axis_size("ctx")
    )
    got = lax.all_to_all(sent, "ctx", 0, 0)
    mine_cols, sent_cols = trunk_parts(place, near_heads, sequence, out_weight)
    got_cols = lax.ppermute(sent_cols, "col", [(i, i ^ 4) for i in cols])
    pair_out = pair_map(
        place, row, got, conv_near, conv_far, trans_row, trans_in, trans_out, sent_cols
    )
    trunk_out = add_parts(mine_cols, got_cols, pair_out).T
    return (trunk_out, pair_out)


def solution(mesh):
    return jax.shard_map(
        per_device,
        mesh=mesh,
        in_specs=(
            P("ctx", None),
            P(),
            P(None, "col"),
            P(None, "col"),
            P(None, "col"),
            P(),
            P(),
            P(),
            P(),
            P(),
            P(),
            P(),
            P(),
            P(),
        ),
        out_specs=(P("ctx", "col"), P("ctx", "col", None)),
        check_vma=False,
    )
```

```python
import functools
import math

import jax
import jax.numpy as jnp
from jax import lax
from jax.experimental import pallas as pl
from jax.experimental.pallas import tpu as pltpu
from jax.sharding import PartitionSpec as P

POOL = 16
HEAD = 192
EPSILON = 1e-06
LAYER_EPSILON = 1e-05
OUTSIDE = -1e30
SCALE = math.log2(math.e) / math.sqrt(HEAD)
bf16 = jnp.bfloat16
f32 = jnp.float32
VMEM = 56 * 2**20


def params(limit=VMEM):
    return pltpu.CompilerParams(vmem_limit_bytes=limit)


def lanes_of(shape):
    return lax.broadcasted_iota(jnp.int32, shape, len(shape) - 1)


def pack_lanes(low, high):
    rolled = pltpu.roll(high, 64, axis=1)
    middle = jnp.where(lanes_of(rolled.shape) < 64, pltpu.roll(low, 128, axis=1), rolled)
    return jnp.concatenate([low[:, :128], middle], axis=1)


def unpack_query(packed):
    wide = pltpu.roll(packed[:, :256].astype(f32), 64, axis=1)
    lane = lanes_of(wide.shape)
    low = jnp.where(lane < 64, 0.0, wide).astype(bf16)
    high = jnp.where(lane < 64, 0.0, packed[:, 128:].astype(f32)).astype(bf16)
    return jnp.concatenate([low, high], axis=0)


def normalised(x, gain):
    square = jnp.mean(x * x, axis=-1, keepdims=True)
    return (x * lax.rsqrt(square + EPSILON) * gain).astype(bf16)


def turned_dot(a, b):
    return lax.dot_general(a, b, (((1,), (1,)), ((), ())), preferred_element_type=f32)


def project_kv_kernel(seq_ref, gain_ref, wk_ref, wv_ref, kv_ref):
    gain = gain_ref[...].astype(f32).reshape(1, -1)
    weights = jnp.concatenate([wv_ref[...], wk_ref[...]], axis=0)
    rows = seq_ref.shape[0]
    part = rows // 2
    for start in range(0, rows, part):
        normed = normalised(seq_ref[start : start + part, :].astype(f32), gain)
        kv_ref[start : start + part, :] = turned_dot(normed, weights).astype(bf16)


def project_kv(sequence, gain, wk, wv):
    rows, feat = sequence.shape
    steps = 2
    whole = lambda a: pl.BlockSpec(a.shape, lambda t: (0,) * a.ndim)
    wk, wv = wk.T, wv.T
    return pl.pallas_call(
        project_kv_kernel,
        grid=(steps,),
        in_specs=[pl.BlockSpec((rows // steps, feat), lambda t: (t, 0)), whole(gain), whole(wk), whole(wv)],
        out_specs=pl.BlockSpec((rows // steps, 2 * HEAD), lambda t: (t, 0)),
        out_shape=jax.ShapeDtypeStruct((rows, 2 * HEAD), bf16),
        compiler_params=params(),
        name="project_kv",
        cost_estimate=pl.CostEstimate(flops=4 * rows * feat * HEAD, bytes_accessed=5_000_000, transcendentals=0),
    )(sequence, gain, wk, wv)


def project_q_kernel(low_ref, high_ref, gain_ref, wq_ref, q_ref, ml_ref, mh_ref):
    gain = gain_ref[...].astype(f32).reshape(1, -1)
    rows = low_ref.shape[0]
    part = rows // 2
    for start in range(0, rows, part):
        halves = []
        for ref, mean_ref in ((low_ref, ml_ref), (high_ref, mh_ref)):
            x = ref[start : start + part, :].astype(f32)
            mean = jnp.mean(x.reshape(part // POOL, POOL, x.shape[1]), axis=1)
            mean_ref[start // POOL : (start + part) // POOL, :] = mean
            halves.append(normalised(x, gain))
        q = turned_dot(jnp.concatenate(halves, axis=0), wq_ref[...]) * SCALE
        q = jnp.concatenate([q, jnp.zeros((2 * part, 64), f32)], axis=1)
        q_ref[start : start + part, :] = pack_lanes(q[:part], q[part:]).astype(bf16)


def project_q(sequence, gain, wq):
    rows, feat = sequence.shape
    steps = 2
    tile = rows // 2 // steps
    whole = lambda a: pl.BlockSpec(a.shape, lambda t: (0,) * a.ndim)
    wq = wq.T
    return pl.pallas_call(
        project_q_kernel,
        grid=(steps,),
        in_specs=[
            pl.BlockSpec((tile, feat), lambda t: (t, 0)),
            pl.BlockSpec((tile, feat), lambda t: (t + steps, 0)),
            whole(gain),
            whole(wq),
        ],
        out_specs=[
            pl.BlockSpec((tile, 2 * HEAD), lambda t: (t, 0)),
            pl.BlockSpec((tile // POOL, feat), lambda t: (t, 0)),
            pl.BlockSpec((tile // POOL, feat), lambda t: (t, 0)),
        ],
        out_shape=[
            jax.ShapeDtypeStruct((rows // 2, 2 * HEAD), bf16),
            jax.ShapeDtypeStruct((rows // 2 // POOL, feat), f32),
            jax.ShapeDtypeStruct((rows // 2 // POOL, feat), f32),
        ],
        compiler_params=params(),
        name="project_q",
        cost_estimate=pl.CostEstimate(flops=2 * rows * feat * HEAD, bytes_accessed=5_000_000, transcendentals=0),
    )(sequence, sequence, gain, wq)


SUB = 256


def log_rows(logs):
    rows = []
    for log in logs:
        for g in range(log.shape[0] // 128):
            block = jnp.broadcast_to(log[g * 128 : (g + 1) * 128], (128, 128))
            rows.append(block.T[:1])
    return jnp.concatenate(rows, axis=0)


def attend_kernel(*refs, count, carried, mode, orders):
    q_ref = refs[0]
    kv_refs = refs[1 : 1 + count]
    rest = list(refs[1 + count :])
    state_ref = rest.pop(0) if carried else None
    rest = rest[orders:]
    out_ref = rest.pop(0)
    log_ref = rest.pop(0) if mode == "final" else None
    v_buf = rest[0]
    queries = unpack_query(q_ref[...])
    subs = queries.shape[0] // SUB
    half = subs // 2
    order = range(subs) if mode == "state" else [i + s * half for i in range(half) for s in range(2)]
    units = [(i, c) for i in order for c in range(count)]
    size = kv_refs[0].shape[0]

    def score(unit):
        i, c = unit
        if i == 0:
            v = kv_refs[c][:, :256]
            lane = lanes_of(v.shape)
            v_buf[c * size : (c + 1) * size, :] = jnp.where(
                lane < HEAD, v, jnp.where(lane == HEAD, 1.0, 0.0).astype(bf16)
            )
        return turned_dot(queries[i * SUB : (i + 1) * SUB], kv_refs[c][:, 128:])

    following = score(units[0])
    results = {}
    top = total = None
    for n, (i, c) in enumerate(units):
        scores = following
        if n + 1 < len(units):
            following = score(units[n + 1])
        here = jnp.max(scores, axis=1, keepdims=True)
        new = here if c == 0 else jnp.maximum(top, here)
        weights = jnp.exp2(scores - new).astype(bf16)
        mixed = jnp.dot(weights, v_buf[c * size : (c + 1) * size, :], preferred_element_type=f32)
        total = mixed if c == 0 else total * jnp.exp2(top - new) + mixed
        top = new
        if c < count - 1:
            continue
        if carried:
            before = state_ref[i * SUB : (i + 1) * SUB, :]
            old = before[:, HEAD + 1 : HEAD + 2]
            new = jnp.maximum(top, old)
            total = total * jnp.exp2(top - new) + before * jnp.exp2(old - new)
            top = new
        if mode == "state":
            out_ref[i * SUB : (i + 1) * SUB, :] = jnp.where(lanes_of(total.shape) == HEAD + 1, top, total)
            continue
        sums = total[:, HEAD : HEAD + 1]
        results[i] = (total * (1.0 / sums), top + jnp.log2(sums))
        if i >= half:
            packed = pack_lanes(results[i - half][0], results[i][0])
            out_ref[(i - half) * SUB : (i - half + 1) * SUB, :] = packed.astype(out_ref.dtype)
    if mode != "state":
        rows = log_rows([results[i][1] for i in range(subs)])
    if mode == "remote":
        rows = jnp.concatenate([rows, jnp.zeros((16 - rows.shape[0], 128), f32)], axis=0)
        first = rows.astype(bf16)
        left = rows - first.astype(f32)
        second = left.astype(bf16)
        third = (left - second.astype(f32)).astype(bf16)
        out_ref[half * SUB :, :] = jnp.concatenate([first, second, third], axis=1)
    if mode == "final":
        log_ref[...] = rows


def attend(query, kvs, state=None, mode="state", orders=()):
    rows = query.shape[0]
    keys = sum(kv.shape[0] for kv in kvs)
    args = [query, *kvs] + ([] if state is None else [state])
    out_shape = {
        "state": [jax.ShapeDtypeStruct((2 * rows, 256), f32)],
        "remote": [jax.ShapeDtypeStruct((rows + 16, 2 * HEAD), bf16)],
        "final": [
            jax.ShapeDtypeStruct((rows, 2 * HEAD), f32),
            jax.ShapeDtypeStruct((2 * rows // 128, 128), f32),
        ],
    }[mode]
    vmem = pl.BlockSpec(memory_space=pltpu.VMEM)
    out = pl.pallas_call(
        functools.partial(
            attend_kernel, count=len(kvs), carried=state is not None, mode=mode, orders=len(orders)
        ),
        in_specs=[vmem] * len(args) + [pl.BlockSpec(memory_space=pl.ANY)] * len(orders),
        out_specs=[vmem] * len(out_shape),
        out_shape=out_shape,
        scratch_shapes=[pltpu.VMEM((keys, 256), bf16)],
        compiler_params=params(36 * 2**20),
        name="attend_" + mode,
        cost_estimate=pl.CostEstimate(
            flops=2 * 2 * rows * keys * 512, bytes_accessed=4_000_000, transcendentals=2 * rows * keys
        ),
    )(*args, *orders)
    return out if mode == "final" else out[0]


def cut_kernel(below_ref, above_ref, *refs):
    out_low_ref, out_high_ref, sems = refs[-3:]
    n = out_low_ref.shape[0]
    low = pltpu.make_async_copy(below_ref.at[pl.ds(0, n)], out_low_ref, sems.at[0])
    high = pltpu.make_async_copy(above_ref.at[pl.ds(n, n)], out_high_ref, sems.at[1])
    low.start()
    high.start()
    low.wait()
    high.wait()


def cut(below, above, *orders):
    hbm = pl.BlockSpec(memory_space=pl.ANY)
    part = jax.ShapeDtypeStruct((below.shape[0] // 2, below.shape[1]), below.dtype)
    return pl.pallas_call(
        cut_kernel,
        in_specs=[hbm] * (2 + len(orders)),
        out_specs=[hbm] * 2,
        out_shape=[part] * 2,
        scratch_shapes=[pltpu.SemaphoreType.DMA((2,))],
        compiler_params=params(2**20),
        name="cut",
    )(below, above, *orders)


def join_kernel(low_ref, high_ref, order_ref, out_ref, sems):
    n = low_ref.shape[0]
    low = pltpu.make_async_copy(low_ref, out_ref.at[pl.ds(0, n)], sems.at[0])
    high = pltpu.make_async_copy(high_ref, out_ref.at[pl.ds(n, n)], sems.at[1])
    low.start()
    high.start()
    low.wait()
    high.wait()


def join(low, high, order):
    hbm = pl.BlockSpec(memory_space=pl.ANY)
    return pl.pallas_call(
        join_kernel,
        in_specs=[hbm] * 3,
        out_specs=hbm,
        out_shape=jax.ShapeDtypeStruct((2 * low.shape[0], low.shape[1]), low.dtype),
        scratch_shapes=[pltpu.SemaphoreType.DMA((2,))],
        compiler_params=params(2**20),
        name="join",
    )(low, high, order)


def relay_kernel(x_ref, *refs):
    out_ref, sem = refs[-2:]
    copy = pltpu.make_async_copy(x_ref, out_ref, sem)
    copy.start()
    copy.wait()


def relay(x, *orders):
    hbm = pl.BlockSpec(memory_space=pl.ANY)
    return pl.pallas_call(
        relay_kernel,
        in_specs=[hbm] * (1 + len(orders)),
        out_specs=hbm,
        out_shape=jax.ShapeDtypeStruct(x.shape, x.dtype),
        scratch_shapes=[pltpu.SemaphoreType.DMA],
        compiler_params=params(2**20),
        name="relay",
    )(x, *orders)


def merge_kernel(mine_ref, log_ref, other_ref, out_ref, pool_ref):
    n = out_ref.shape[0]
    stats = other_ref[n:, :].astype(f32)
    rows = (stats[:, :128] + stats[:, 128:256] + stats[:, 256:])[: 2 * n // 128]
    share = 1.0 / (1.0 + jnp.exp2(log_ref[...] - rows))
    columns = []
    for g in range(2 * n // 128):
        columns.append(jnp.broadcast_to(share[g : g + 1], (128, 128)).T)
    low = jnp.concatenate(columns[: n // 128], axis=0)
    high = jnp.concatenate(columns[n // 128 :], axis=0)
    middle = jnp.where(lanes_of(low.shape) < 64, low, high)
    share = jnp.concatenate([low, middle, high], axis=1)
    mine = mine_ref[...]
    attended = (mine + share * (other_ref[:n, :].astype(f32) - mine)).astype(bf16)
    out_ref[...] = attended
    wide = attended.astype(f32)
    pool = jnp.mean(wide.reshape(n // POOL, POOL, wide.shape[1]), axis=1).astype(bf16)
    for k in range(pool_ref.shape[0]):
        pool_ref[k] = pool


def merge(mine, log, other):
    rows = mine.shape[0]
    vmem = pl.BlockSpec(memory_space=pltpu.VMEM)
    return pl.pallas_call(
        merge_kernel,
        in_specs=[vmem] * 3,
        out_specs=[vmem] * 2,
        out_shape=[
            jax.ShapeDtypeStruct((rows, 2 * HEAD), bf16),
            jax.ShapeDtypeStruct((8, rows // POOL, 2 * HEAD), bf16),
        ],
        compiler_params=params(16 * 2**20),
        name="merge",
    )(mine, log, other)


def features_kernel(*refs):
    sources, rest = refs[:7], refs[7:]
    rout_ref, sent_ref, pool_ref, ml_ref, mh_ref, w_ref, gain_ref, row_ref, col_ref, sems = rest
    held = (pool_ref, ml_ref, mh_ref, w_ref, gain_ref, row_ref, col_ref)
    parts = 6
    depth = w_ref.shape[0] // parts
    copies = {}
    for n in (0, 3, 1, 2, 4, 5, 6):
        if n == 3:
            w_copies = []
            for p in range(parts):
                piece = pl.ds(p * depth, depth)
                w_copies.append(pltpu.make_async_copy(sources[3].at[piece], w_ref.at[piece], sems.at[p]))
                w_copies[p].start()
        else:
            copies[n] = pltpu.make_async_copy(sources[n], held[n], sems.at[parts + n])
            copies[n].start()
    copies[0].wait()
    heads = []
    for h in range(8):
        packed = pool_ref[h].astype(f32)
        low, high = packed[:, :256], pltpu.roll(packed[:, 128:], 192, axis=1)
        heads.append(jnp.concatenate([low, high], axis=0)[:, :HEAD])
    lhs = jnp.concatenate(heads, axis=1).astype(bf16)
    pooled = None
    for p in range(parts):
        w_copies[p].wait()
        piece = slice(p * depth, (p + 1) * depth)
        product = jnp.dot(lhs[:, piece], w_ref[piece, :], preferred_element_type=f32)
        pooled = product if pooled is None else pooled + product
    for n in (1, 2, 4, 5, 6):
        copies[n].wait()
    pooled = pooled + jnp.concatenate([ml_ref[...], mh_ref[...]], axis=0)
    inverse = lax.rsqrt(jnp.mean(pooled * pooled, axis=-1, keepdims=True) + EPSILON)
    scaled = (pooled * gain_ref[...].astype(f32)).astype(bf16)
    weights = jnp.concatenate([row_ref[...], col_ref[...]], axis=1)
    got = (inverse * jnp.dot(scaled, weights, preferred_element_type=f32)).astype(bf16).astype(f32)
    channels = rout_ref.shape[1]
    row, col = got[:, :channels], got[:, channels:]
    rout_ref[...] = row.astype(bf16)
    sent = jnp.concatenate([col, row[:8], row[-8:]], axis=0).astype(bf16)
    for k in range(sent_ref.shape[0]):
        sent_ref[k] = sent


def features(pools, mean_low, mean_high, out_weight, gain, row_weight, column_weight, copies):
    rows = 2 * mean_low.shape[0]
    channels = row_weight.shape[1]
    vmem = pl.BlockSpec(memory_space=pltpu.VMEM)
    hbm = pl.BlockSpec(memory_space=pl.ANY)
    return pl.pallas_call(
        features_kernel,
        in_specs=[hbm] * 7,
        out_specs=[vmem] * 2,
        out_shape=[
            jax.ShapeDtypeStruct((rows, channels), bf16),
            jax.ShapeDtypeStruct((copies, rows + 16, channels), bf16),
        ],
        scratch_shapes=[
            pltpu.VMEM(a.shape, a.dtype)
            for a in (pools, mean_low, mean_high, out_weight, gain, row_weight, column_weight)
        ]
        + [pltpu.SemaphoreType.DMA((13,))],
        compiler_params=params(),
        name="features",
    )(pools, mean_low, mean_high, out_weight, gain, row_weight, column_weight)


def pair_kernel(
    place_ref, row_ref, got_ref, near_ref, far_ref, gain_ref, in_ref, tout_ref, order_ref,
    out_ref, row_buf, col_buf, wn_ref, wf_ref, xn_ref, xf_ref, first_ref, second_ref,
):
    rows, cols, channels = out_ref.shape
    ctx, col = place_ref[0], place_ref[1]
    gone = jnp.full((8, channels), OUTSIDE, f32)
    spots = got_ref.shape[0]
    above = got_ref[jnp.maximum(ctx - 1, 0)][rows + 8 :].astype(f32)
    below = got_ref[jnp.minimum(ctx + 1, spots - 1)][rows : rows + 8].astype(f32)
    row_buf[:8] = jnp.where(ctx == 0, gone, above)
    row_buf[8 : 8 + rows] = row_ref[...].astype(f32)
    row_buf[8 + rows :] = jnp.where(ctx == spots - 1, gone, below)
    half = cols // 2
    left = got_ref[jnp.maximum(2 * col - 1, 0)][half - 8 : half].astype(f32)
    right = got_ref[jnp.minimum(2 * col + 2, spots - 1)][:8].astype(f32)
    col_buf[:8] = jnp.where(col == 0, gone, left)
    col_buf[8 : 8 + half] = got_ref[2 * col][:half].astype(f32)
    col_buf[8 + half : 8 + cols] = got_ref[2 * col + 1][:half].astype(f32)
    col_buf[8 + cols :] = jnp.where(2 * col + 2 >= spots, gone, right)

    blank = jnp.zeros((channels, channels), bf16)
    for kernel_ref, w_ref in ((near_ref, wn_ref), (far_ref, wf_ref)):
        for a in range(4):
            for b in range(3):
                at = (a * 3 + b) * channels
                w_ref[at : at + channels, :channels] = kernel_ref[a, b] if a < 3 else blank
                w_ref[at : at + channels, channels:] = kernel_ref[a - 1, b] if a > 0 else blank

    span = cols + 8
    shifted = [col_buf[2 + 2 * b : 2 + 2 * b + span, :] for b in range(3)]
    taps = jnp.concatenate(shifted, axis=1)

    def fill(r):
        row = row_buf[pl.ds(r + 2, 1), :]
        triple = jnp.concatenate([row, row, row], axis=1)
        xn_ref[r] = jnp.maximum(triple + taps, 0.0).astype(bf16)

    def near_step(g):
        start = g * 8
        lhs = []
        for k in (0, 1, 4, 5):
            lhs.append(jnp.concatenate([xn_ref[start + k + 2 * a] for a in range(4)], axis=1))
        got = jnp.dot(jnp.concatenate(lhs, axis=0), wn_ref[...], preferred_element_type=f32)
        for n, k in enumerate((0, 1, 4, 5)):
            for side in range(2):
                r = start + k + 2 * side
                part = got[n * span : (n + 1) * span, side * channels : (side + 1) * channels]
                first = part + row_buf[pl.ds(r + 4, 1), :] + shifted[1]
                centre = first[4 : 4 + cols]
                first_ref[r] = centre
                hidden = jnp.concatenate([first[:cols], centre, first[8 : 8 + cols]], axis=1)
                xf_ref[r] = jnp.maximum(hidden, 0.0).astype(bf16)

    def far_step(g):
        start = g * 8
        lhs = []
        for k in range(4):
            lhs.append(jnp.concatenate([xf_ref[start + k + 4 * a] for a in range(4)], axis=1))
        got = jnp.dot(jnp.concatenate(lhs, axis=0), wf_ref[...], preferred_element_type=f32)
        for side in range(2):
            for k in range(4):
                part = got[k * cols : (k + 1) * cols, side * channels : (side + 1) * channels]
                second_ref[4 * side + k] = part + first_ref[start + 4 * side + k + 4]

    def transition_step(g):
        start = g * 8
        second = second_ref[...].reshape(8 * cols, channels)
        centred = second - jnp.mean(second, axis=-1, keepdims=True)
        variance = jnp.mean(centred * centred, axis=-1, keepdims=True)
        layer = (centred * lax.rsqrt(variance + LAYER_EPSILON) * gain_ref[...].astype(f32)).astype(bf16)
        middle = jnp.dot(layer, in_ref[...], preferred_element_type=f32)
        middle = jnp.maximum(middle, 0.0).astype(bf16)
        result = (second + jnp.dot(middle, tout_ref[...], preferred_element_type=f32)).astype(bf16)
        for k in range(8):
            out_ref[start + k] = result[k * cols : (k + 1) * cols]

    last = rows // 8
    for r in range(12):
        fill(r)

    def fill_for(g):
        for r in range(8):
            fill(g * 8 + 4 + r)

    near_step(0)
    fill_for(1)
    near_step(1)
    fill_for(2)
    far_step(0)
    near_step(2)
    fill_for(3)

    def steady(g, carry):
        near_step(g)
        transition_step(g - 3)
        far_step(g - 2)

        @pl.when(g < last)
        def _():
            fill_for(g + 1)

        return carry

    lax.fori_loop(3, last + 1, steady, 0)
    transition_step(last - 2)
    far_step(last - 1)
    transition_step(last - 1)


def pair_map(place, row, got, near, far, gain, trans_in, trans_out, order):
    rows, channels = row.shape
    cols = 2 * rows
    vmem = pl.BlockSpec(memory_space=pltpu.VMEM)
    return pl.pallas_call(
        pair_kernel,
        in_specs=[pl.BlockSpec(memory_space=pltpu.SMEM)] + [vmem] * 7 + [pl.BlockSpec(memory_space=pl.ANY)],
        out_specs=vmem,
        out_shape=jax.ShapeDtypeStruct((rows, cols, channels), bf16),
        scratch_shapes=[
            pltpu.VMEM((rows + 16, channels), f32),
            pltpu.VMEM((cols + 16, channels), f32),
            pltpu.VMEM((12 * channels, 2 * channels), bf16),
            pltpu.VMEM((12 * channels, 2 * channels), bf16),
            pltpu.VMEM((rows + 12, cols + 8, 3 * channels), bf16),
            pltpu.VMEM((rows + 8, cols, 3 * channels), bf16),
            pltpu.VMEM((rows + 8, cols, channels), f32),
            pltpu.VMEM((8, cols, channels), f32),
        ],
        compiler_params=params(),
        name="pair_map",
        cost_estimate=pl.CostEstimate(flops=14_000_000_000, bytes_accessed=3_000_000, transcendentals=0),
    )(place, row, got, near, far, gain, trans_in, trans_out, order)


def trunk_kernel(place_ref, near_hbm, seq_hbm, w_hbm, mine_ref, sent_ref, all_buf, seq_buf, wl_buf, wh_buf, turned, sems):
    n = all_buf.shape[1]
    col = place_ref[1]
    other = lax.rem(col + 4, 8)
    windows = [pl.ds(pl.multiple_of((c * 3 // 2) * 128, 128), 256) for c in (col, other)]
    seq_copy = pltpu.make_async_copy(seq_hbm.at[:, windows[0]], seq_buf, sems.at[0])
    copies = []
    for h in range(4):
        row = pl.multiple_of((col // 4 * 4 + h) * HEAD, HEAD)
        copies.append(pltpu.make_async_copy(near_hbm.at[pl.ds(h * n, n)], all_buf.at[h], sems.at[1 + 5 * h]))
        for k, window in enumerate(windows):
            weight = w_hbm.at[pl.ds(row, HEAD), window]
            low = wl_buf.at[pl.ds(h * 256, HEAD), pl.ds(256 * k, 256)]
            high = wh_buf.at[pl.ds(h * 256 + 64, HEAD), pl.ds(256 * k, 256)]
            copies.append(pltpu.make_async_copy(weight, low, sems.at[2 + 5 * h + 2 * k]))
            copies.append(pltpu.make_async_copy(weight, high, sems.at[3 + 5 * h + 2 * k]))
    for copy in copies:
        copy.start()
    seq_copy.start()
    for h in range(4):
        wl_buf[h * 256 + HEAD : (h + 1) * 256, :] = jnp.zeros((64, 512), bf16)
        wh_buf[h * 256 : h * 256 + 64, :] = jnp.zeros((64, 512), bf16)
    for copy in copies:
        copy.wait()
    seq_copy.wait()
    for side, w_buf in ((0, wl_buf), (1, wh_buf)):
        lhs = jnp.concatenate([all_buf[h][:, 128 * side : 128 * side + 256] for h in range(4)], axis=1)
        part = jnp.dot(lhs, w_buf[...], preferred_element_type=f32)
        at = slice(side * n, (side + 1) * n)
        turned[:256, at] = (part[:, :256] + seq_buf[at, :].astype(f32)).T
        turned[256:, at] = part[:, 256:].T
    offset = pl.multiple_of(lax.rem(col, 2) * 64, 64)
    mine_ref[...] = turned[pl.ds(offset, HEAD), :]
    sent_ref[...] = turned[pl.ds(pl.multiple_of(256 + offset, 64), HEAD), :].astype(bf16)


def trunk_parts(place, near, sequence, out_weight):
    vmem = pl.BlockSpec(memory_space=pltpu.VMEM)
    hbm = pl.BlockSpec(memory_space=pl.ANY)
    rows = sequence.shape[0]
    return pl.pallas_call(
        trunk_kernel,
        in_specs=[pl.BlockSpec(memory_space=pltpu.SMEM)] + [hbm] * 3,
        out_specs=[vmem] * 2,
        out_shape=[jax.ShapeDtypeStruct((HEAD, rows), f32), jax.ShapeDtypeStruct((HEAD, rows), bf16)],
        scratch_shapes=[
            pltpu.VMEM((4, rows // 2, 2 * HEAD), bf16),
            pltpu.VMEM((rows, 256), bf16),
            pltpu.VMEM((4 * 256, 512), bf16),
            pltpu.VMEM((4 * 256, 512), bf16),
            pltpu.VMEM((512, rows), f32),
            pltpu.SemaphoreType.DMA((21,)),
        ],
        compiler_params=params(),
        name="trunk_parts",
        cost_estimate=pl.CostEstimate(flops=1_100_000_000, bytes_accessed=5_000_000, transcendentals=0),
    )(place, near, sequence, out_weight)


def per_device(
    sequence,
    norm_gain,
    query_weight,
    key_weight,
    value_weight,
    out_weight,
    pool_gain,
    row_weight,
    column_weight,
    conv_near,
    conv_far,
    trans_gain,
    trans_in,
    trans_out,
):
    place = jnp.stack([lax.axis_index("ctx"), lax.axis_index("col")]).astype(jnp.int32)
    spots = range(16)
    cols = range(8)
    to_core = [(i, i ^ 1) for i in spots]
    to_z = [(i, i ^ 8) for i in spots]
    to_up = [(i, (i & 8) | ((i + 2) & 7)) for i in spots]
    to_down = [(i, (i & 8) | ((i - 2) & 7)) for i in spots]

    def send(x, perm):
        return lax.ppermute(x, "ctx", perm)

    kv = project_kv(sequence, norm_gain, key_weight, value_weight)
    kv_core = send(kv, to_core)
    kv_below = send(kv, to_up)
    kv_above = send(kv, to_down)
    query, mean_low, mean_high = project_q(sequence, norm_gain, query_weight)
    query_z = send(query, to_z)
    state = attend(query, [kv, kv_core])
    gain_row = pool_gain.reshape(1, -1)
    trans_row = trans_gain.reshape(1, -1)
    low, high = cut(kv_below, kv_above, state)
    far_below = send(low, to_up)
    far_above = send(high, to_down)
    twin = [send(kv_below, to_core), send(kv_above, to_core)]
    state_z = attend(query_z, [kv, kv_core, kv_below, kv_above], orders=(low, gain_row, trans_row, place))
    opposite = join(far_below, far_above, state_z)
    opposite_core = send(opposite, to_core)
    state_z = attend(query_z, twin, state_z)
    returned = attend(query_z, [opposite, opposite_core], state_z, mode="remote")
    other = send(returned, to_z)
    rest = [kv_below, kv_above, *twin, opposite, opposite_core]
    mine, log = attend(query, rest, state, mode="final")
    attended, pool = merge(mine, log, other)

    along_y = [[0, 1, 2, 3], [4, 5, 6, 7]]
    near_heads = lax.all_gather(attended, "col", axis=0, tiled=True, axis_index_groups=along_y)
    pools = lax.all_to_all(pool, "col", 0, 0)
    row, sent = features(
        pools, mean_low, mean_high, out_weight, gain_row, row_weight, column_weight, lax.axis_size("ctx")
    )
    got = lax.all_to_all(sent, "ctx", 0, 0)
    mine_cols, sent_cols = trunk_parts(place, near_heads, sequence, out_weight)
    got_cols = lax.ppermute(sent_cols, "col", [(i, i ^ 4) for i in cols])
    pair_out = pair_map(
        place, row, got, conv_near, conv_far, trans_row, trans_in, trans_out, sent_cols
    )
    trunk_out = (mine_cols + got_cols.astype(f32)).astype(bf16).T
    return (trunk_out, pair_out)


def solution(mesh):
    return jax.shard_map(
        per_device,
        mesh=mesh,
        in_specs=(
            P("ctx", None),
            P(),
            P(None, "col"),
            P(None, "col"),
            P(None, "col"),
            P(),
            P(),
            P(),
            P(),
            P(),
            P(),
            P(),
            P(),
            P(),
        ),
        out_specs=(P("ctx", "col"), P("ctx", "col", None)),
        check_vma=False,
    )
```

```python
import functools
import math

import jax
import jax.numpy as jnp
from jax import lax
from jax.experimental import pallas as pl
from jax.experimental.pallas import tpu as pltpu
from jax.sharding import PartitionSpec as P

POOL = 16
HEAD = 192
EPSILON = 1e-06
LAYER_EPSILON = 1e-05
OUTSIDE = -1e30
SCALE = math.log2(math.e) / math.sqrt(HEAD)
bf16 = jnp.bfloat16
f32 = jnp.float32
VMEM = 56 * 2**20


def params(limit=VMEM):
    return pltpu.CompilerParams(vmem_limit_bytes=limit)


def lanes_of(shape):
    return lax.broadcasted_iota(jnp.int32, shape, len(shape) - 1)


def pack_lanes(low, high):
    rolled = pltpu.roll(high, 64, axis=1)
    middle = jnp.where(lanes_of(rolled.shape) < 64, pltpu.roll(low, 128, axis=1), rolled)
    return jnp.concatenate([low[:, :128], middle], axis=1)


def unpack_query(packed):
    wide = pltpu.roll(packed[:, :256].astype(f32), 64, axis=1)
    lane = lanes_of(wide.shape)
    low = jnp.where(lane < 64, 0.0, wide).astype(bf16)
    high = jnp.where(lane < 64, 0.0, packed[:, 128:].astype(f32)).astype(bf16)
    return jnp.concatenate([low, high], axis=0)


def normalised(x, gain):
    square = jnp.mean(x * x, axis=-1, keepdims=True)
    return (x * lax.rsqrt(square + EPSILON) * gain).astype(bf16)


def turned_dot(a, b):
    return lax.dot_general(a, b, (((1,), (1,)), ((), ())), preferred_element_type=f32)


def project_kv_kernel(seq_ref, gain_ref, wk_ref, wv_ref, kv_ref):
    gain = gain_ref[...].astype(f32).reshape(1, -1)
    weights = jnp.concatenate([wv_ref[...], wk_ref[...]], axis=0)
    rows = seq_ref.shape[0]
    part = rows // 2
    for start in range(0, rows, part):
        normed = normalised(seq_ref[start : start + part, :].astype(f32), gain)
        kv_ref[start : start + part, :] = turned_dot(normed, weights).astype(bf16)


def project_kv(sequence, gain, wk, wv):
    rows, feat = sequence.shape
    steps = 2
    whole = lambda a: pl.BlockSpec(a.shape, lambda t: (0,) * a.ndim)
    wk, wv = wk.T, wv.T
    return pl.pallas_call(
        project_kv_kernel,
        grid=(steps,),
        in_specs=[pl.BlockSpec((rows // steps, feat), lambda t: (t, 0)), whole(gain), whole(wk), whole(wv)],
        out_specs=pl.BlockSpec((rows // steps, 2 * HEAD), lambda t: (t, 0)),
        out_shape=jax.ShapeDtypeStruct((rows, 2 * HEAD), bf16),
        compiler_params=params(),
        name="project_kv",
        cost_estimate=pl.CostEstimate(flops=4 * rows * feat * HEAD, bytes_accessed=5_000_000, transcendentals=0),
    )(sequence, gain, wk, wv)


def project_q_kernel(low_ref, high_ref, gain_ref, wq_ref, q_ref, ml_ref, mh_ref):
    gain = gain_ref[...].astype(f32).reshape(1, -1)
    rows = low_ref.shape[0]
    part = rows // 2
    for start in range(0, rows, part):
        halves = []
        for ref, mean_ref in ((low_ref, ml_ref), (high_ref, mh_ref)):
            x = ref[start : start + part, :].astype(f32)
            mean = jnp.mean(x.reshape(part // POOL, POOL, x.shape[1]), axis=1)
            mean_ref[start // POOL : (start + part) // POOL, :] = mean
            halves.append(normalised(x, gain))
        q = turned_dot(jnp.concatenate(halves, axis=0), wq_ref[...]) * SCALE
        q = jnp.concatenate([q, jnp.zeros((2 * part, 64), f32)], axis=1)
        q_ref[start : start + part, :] = pack_lanes(q[:part], q[part:]).astype(bf16)


def project_q(sequence, gain, wq):
    rows, feat = sequence.shape
    steps = 2
    tile = rows // 2 // steps
    whole = lambda a: pl.BlockSpec(a.shape, lambda t: (0,) * a.ndim)
    wq = wq.T
    return pl.pallas_call(
        project_q_kernel,
        grid=(steps,),
        in_specs=[
            pl.BlockSpec((tile, feat), lambda t: (t, 0)),
            pl.BlockSpec((tile, feat), lambda t: (t + steps, 0)),
            whole(gain),
            whole(wq),
        ],
        out_specs=[
            pl.BlockSpec((tile, 2 * HEAD), lambda t: (t, 0)),
            pl.BlockSpec((tile // POOL, feat), lambda t: (t, 0)),
            pl.BlockSpec((tile // POOL, feat), lambda t: (t, 0)),
        ],
        out_shape=[
            jax.ShapeDtypeStruct((rows // 2, 2 * HEAD), bf16),
            jax.ShapeDtypeStruct((rows // 2 // POOL, feat), f32),
            jax.ShapeDtypeStruct((rows // 2 // POOL, feat), f32),
        ],
        compiler_params=params(),
        name="project_q",
        cost_estimate=pl.CostEstimate(flops=2 * rows * feat * HEAD, bytes_accessed=5_000_000, transcendentals=0),
    )(sequence, sequence, gain, wq)


SUB = 256


def log_rows(logs):
    rows = []
    for log in logs:
        for g in range(log.shape[0] // 128):
            block = jnp.broadcast_to(log[g * 128 : (g + 1) * 128], (128, 128))
            rows.append(block.T[:1])
    return jnp.concatenate(rows, axis=0)


def attend_kernel(*refs, count, carried, mode, orders):
    q_ref = refs[0]
    kv_refs = refs[1 : 1 + count]
    rest = list(refs[1 + count :])
    state_ref = rest.pop(0) if carried else None
    rest = rest[orders:]
    out_ref = rest.pop(0)
    log_ref = rest.pop(0) if mode == "final" else None
    v_buf = rest[0]
    queries = unpack_query(q_ref[...])
    subs = queries.shape[0] // SUB
    half = subs // 2
    order = range(subs) if mode == "state" else [i + s * half for i in range(half) for s in range(2)]
    units = [(i, c) for i in order for c in range(count)]
    size = kv_refs[0].shape[0]

    def score(unit):
        i, c = unit
        if i == 0:
            v = kv_refs[c][:, :256]
            lane = lanes_of(v.shape)
            v_buf[c * size : (c + 1) * size, :] = jnp.where(
                lane < HEAD, v, jnp.where(lane == HEAD, 1.0, 0.0).astype(bf16)
            )
        return turned_dot(queries[i * SUB : (i + 1) * SUB], kv_refs[c][:, 128:])

    following = score(units[0])
    results = {}
    top = total = None
    for n, (i, c) in enumerate(units):
        scores = following
        if n + 1 < len(units):
            following = score(units[n + 1])
        here = jnp.max(scores, axis=1, keepdims=True)
        new = here if c == 0 else jnp.maximum(top, here)
        weights = jnp.exp2(scores - new).astype(bf16)
        mixed = jnp.dot(weights, v_buf[c * size : (c + 1) * size, :], preferred_element_type=f32)
        total = mixed if c == 0 else total * jnp.exp2(top - new) + mixed
        top = new
        if c < count - 1:
            continue
        if carried:
            before = state_ref[i * SUB : (i + 1) * SUB, :]
            old = before[:, HEAD + 1 : HEAD + 2]
            new = jnp.maximum(top, old)
            total = total * jnp.exp2(top - new) + before * jnp.exp2(old - new)
            top = new
        if mode == "state":
            out_ref[i * SUB : (i + 1) * SUB, :] = jnp.where(lanes_of(total.shape) == HEAD + 1, top, total)
            continue
        sums = total[:, HEAD : HEAD + 1]
        results[i] = (total * (1.0 / sums), top + jnp.log2(sums))
        if i >= half:
            packed = pack_lanes(results[i - half][0], results[i][0])
            out_ref[(i - half) * SUB : (i - half + 1) * SUB, :] = packed.astype(out_ref.dtype)
    if mode != "state":
        rows = log_rows([results[i][1] for i in range(subs)])
    if mode == "remote":
        rows = jnp.concatenate([rows, jnp.zeros((16 - rows.shape[0], 128), f32)], axis=0)
        first = rows.astype(bf16)
        left = rows - first.astype(f32)
        second = left.astype(bf16)
        third = (left - second.astype(f32)).astype(bf16)
        out_ref[half * SUB :, :] = jnp.concatenate([first, second, third], axis=1)
    if mode == "final":
        log_ref[...] = rows


def attend(query, kvs, state=None, mode="state", orders=()):
    rows = query.shape[0]
    keys = sum(kv.shape[0] for kv in kvs)
    args = [query, *kvs] + ([] if state is None else [state])
    out_shape = {
        "state": [jax.ShapeDtypeStruct((2 * rows, 256), f32)],
        "remote": [jax.ShapeDtypeStruct((rows + 16, 2 * HEAD), bf16)],
        "final": [
            jax.ShapeDtypeStruct((rows, 2 * HEAD), f32),
            jax.ShapeDtypeStruct((2 * rows // 128, 128), f32),
        ],
    }[mode]
    vmem = pl.BlockSpec(memory_space=pltpu.VMEM)
    out = pl.pallas_call(
        functools.partial(
            attend_kernel, count=len(kvs), carried=state is not None, mode=mode, orders=len(orders)
        ),
        in_specs=[vmem] * len(args) + [pl.BlockSpec(memory_space=pl.ANY)] * len(orders),
        out_specs=[vmem] * len(out_shape),
        out_shape=out_shape,
        scratch_shapes=[pltpu.VMEM((keys, 256), bf16)],
        compiler_params=params(36 * 2**20),
        name="attend_" + mode,
        cost_estimate=pl.CostEstimate(
            flops=2 * 2 * rows * keys * 512, bytes_accessed=4_000_000, transcendentals=2 * rows * keys
        ),
    )(*args, *orders)
    return out if mode == "final" else out[0]


def cut_kernel(below_ref, above_ref, *refs):
    out_low_ref, out_high_ref, sems = refs[-3:]
    n = out_low_ref.shape[0]
    low = pltpu.make_async_copy(below_ref.at[pl.ds(0, n)], out_low_ref, sems.at[0])
    high = pltpu.make_async_copy(above_ref.at[pl.ds(n, n)], out_high_ref, sems.at[1])
    low.start()
    high.start()
    low.wait()
    high.wait()


def cut(below, above, *orders):
    hbm = pl.BlockSpec(memory_space=pl.ANY)
    part = jax.ShapeDtypeStruct((below.shape[0] // 2, below.shape[1]), below.dtype)
    return pl.pallas_call(
        cut_kernel,
        in_specs=[hbm] * (2 + len(orders)),
        out_specs=[hbm] * 2,
        out_shape=[part] * 2,
        scratch_shapes=[pltpu.SemaphoreType.DMA((2,))],
        compiler_params=params(2**20),
        name="cut",
    )(below, above, *orders)


def join_kernel(low_ref, high_ref, order_ref, out_ref, sems):
    n = low_ref.shape[0]
    low = pltpu.make_async_copy(low_ref, out_ref.at[pl.ds(0, n)], sems.at[0])
    high = pltpu.make_async_copy(high_ref, out_ref.at[pl.ds(n, n)], sems.at[1])
    low.start()
    high.start()
    low.wait()
    high.wait()


def join(low, high, order):
    hbm = pl.BlockSpec(memory_space=pl.ANY)
    return pl.pallas_call(
        join_kernel,
        in_specs=[hbm] * 3,
        out_specs=hbm,
        out_shape=jax.ShapeDtypeStruct((2 * low.shape[0], low.shape[1]), low.dtype),
        scratch_shapes=[pltpu.SemaphoreType.DMA((2,))],
        compiler_params=params(2**20),
        name="join",
    )(low, high, order)


def relay_kernel(x_ref, *refs):
    out_ref, sem = refs[-2:]
    copy = pltpu.make_async_copy(x_ref, out_ref, sem)
    copy.start()
    copy.wait()


def relay(x, *orders):
    hbm = pl.BlockSpec(memory_space=pl.ANY)
    return pl.pallas_call(
        relay_kernel,
        in_specs=[hbm] * (1 + len(orders)),
        out_specs=hbm,
        out_shape=jax.ShapeDtypeStruct(x.shape, x.dtype),
        scratch_shapes=[pltpu.SemaphoreType.DMA],
        compiler_params=params(2**20),
        name="relay",
    )(x, *orders)


def merge_kernel(mine_ref, log_ref, other_ref, out_ref, pool_ref):
    n = out_ref.shape[0]
    stats = other_ref[n:, :].astype(f32)
    rows = (stats[:, :128] + stats[:, 128:256] + stats[:, 256:])[: 2 * n // 128]
    share = 1.0 / (1.0 + jnp.exp2(log_ref[...] - rows))
    columns = []
    for g in range(2 * n // 128):
        columns.append(jnp.broadcast_to(share[g : g + 1], (128, 128)).T)
    low = jnp.concatenate(columns[: n // 128], axis=0)
    high = jnp.concatenate(columns[n // 128 :], axis=0)
    middle = jnp.where(lanes_of(low.shape) < 64, low, high)
    share = jnp.concatenate([low, middle, high], axis=1)
    mine = mine_ref[...]
    attended = (mine + share * (other_ref[:n, :].astype(f32) - mine)).astype(bf16)
    out_ref[...] = attended
    wide = attended.astype(f32)
    pool = jnp.mean(wide.reshape(n // POOL, POOL, wide.shape[1]), axis=1).astype(bf16)
    for k in range(pool_ref.shape[0]):
        pool_ref[k] = pool


def merge(mine, log, other):
    rows = mine.shape[0]
    vmem = pl.BlockSpec(memory_space=pltpu.VMEM)
    return pl.pallas_call(
        merge_kernel,
        in_specs=[vmem] * 3,
        out_specs=[vmem] * 2,
        out_shape=[
            jax.ShapeDtypeStruct((rows, 2 * HEAD), bf16),
            jax.ShapeDtypeStruct((8, rows // POOL, 2 * HEAD), bf16),
        ],
        compiler_params=params(16 * 2**20),
        name="merge",
    )(mine, log, other)


def features_kernel(*refs):
    sources, rest = refs[:7], refs[7:]
    rout_ref, sent_ref, pool_ref, ml_ref, mh_ref, w_ref, gain_ref, row_ref, col_ref, sems = rest
    held = (pool_ref, ml_ref, mh_ref, w_ref, gain_ref, row_ref, col_ref)
    parts = 6
    depth = w_ref.shape[0] // parts
    copies = {}
    for n in (0, 3, 1, 2, 4, 5, 6):
        if n == 3:
            w_copies = []
            for p in range(parts):
                piece = pl.ds(p * depth, depth)
                w_copies.append(pltpu.make_async_copy(sources[3].at[piece], w_ref.at[piece], sems.at[p]))
                w_copies[p].start()
        else:
            copies[n] = pltpu.make_async_copy(sources[n], held[n], sems.at[parts + n])
            copies[n].start()
    copies[0].wait()
    heads = []
    for h in range(8):
        packed = pool_ref[h].astype(f32)
        low, high = packed[:, :256], pltpu.roll(packed[:, 128:], 192, axis=1)
        heads.append(jnp.concatenate([low, high], axis=0)[:, :HEAD])
    lhs = jnp.concatenate(heads, axis=1).astype(bf16)
    pooled = None
    for p in range(parts):
        w_copies[p].wait()
        piece = slice(p * depth, (p + 1) * depth)
        product = jnp.dot(lhs[:, piece], w_ref[piece, :], preferred_element_type=f32)
        pooled = product if pooled is None else pooled + product
    for n in (1, 2, 4, 5, 6):
        copies[n].wait()
    pooled = pooled + jnp.concatenate([ml_ref[...], mh_ref[...]], axis=0)
    inverse = lax.rsqrt(jnp.mean(pooled * pooled, axis=-1, keepdims=True) + EPSILON)
    scaled = (pooled * gain_ref[...].astype(f32)).astype(bf16)
    weights = jnp.concatenate([row_ref[...], col_ref[...]], axis=1)
    got = (inverse * jnp.dot(scaled, weights, preferred_element_type=f32)).astype(bf16).astype(f32)
    channels = rout_ref.shape[1]
    row, col = got[:, :channels], got[:, channels:]
    rout_ref[...] = row.astype(bf16)
    sent = jnp.concatenate([col, row[:8], row[-8:]], axis=0).astype(bf16)
    for k in range(sent_ref.shape[0]):
        sent_ref[k] = sent


def features(pools, mean_low, mean_high, out_weight, gain, row_weight, column_weight, copies):
    rows = 2 * mean_low.shape[0]
    channels = row_weight.shape[1]
    vmem = pl.BlockSpec(memory_space=pltpu.VMEM)
    hbm = pl.BlockSpec(memory_space=pl.ANY)
    return pl.pallas_call(
        features_kernel,
        in_specs=[hbm] * 7,
        out_specs=[vmem] * 2,
        out_shape=[
            jax.ShapeDtypeStruct((rows, channels), bf16),
            jax.ShapeDtypeStruct((copies, rows + 16, channels), bf16),
        ],
        scratch_shapes=[
            pltpu.VMEM(a.shape, a.dtype)
            for a in (pools, mean_low, mean_high, out_weight, gain, row_weight, column_weight)
        ]
        + [pltpu.SemaphoreType.DMA((13,))],
        compiler_params=params(),
        name="features",
    )(pools, mean_low, mean_high, out_weight, gain, row_weight, column_weight)


def pair_kernel(
    place_ref, row_ref, got_ref, near_ref, far_ref, gain_ref, in_ref, tout_ref, order_ref,
    out_ref, row_buf, col_buf, wn_ref, wf_ref, xn_ref, xf_ref, first_ref, second_ref,
):
    rows, cols, channels = out_ref.shape
    ctx, col = place_ref[0], place_ref[1]
    gone = jnp.full((8, channels), OUTSIDE, f32)
    spots = got_ref.shape[0]
    above = got_ref[jnp.maximum(ctx - 1, 0)][rows + 8 :].astype(f32)
    below = got_ref[jnp.minimum(ctx + 1, spots - 1)][rows : rows + 8].astype(f32)
    row_buf[:8] = jnp.where(ctx == 0, gone, above)
    row_buf[8 : 8 + rows] = row_ref[...].astype(f32)
    row_buf[8 + rows :] = jnp.where(ctx == spots - 1, gone, below)
    half = cols // 2
    left = got_ref[jnp.maximum(2 * col - 1, 0)][half - 8 : half].astype(f32)
    right = got_ref[jnp.minimum(2 * col + 2, spots - 1)][:8].astype(f32)
    col_buf[:8] = jnp.where(col == 0, gone, left)
    col_buf[8 : 8 + half] = got_ref[2 * col][:half].astype(f32)
    col_buf[8 + half : 8 + cols] = got_ref[2 * col + 1][:half].astype(f32)
    col_buf[8 + cols :] = jnp.where(2 * col + 2 >= spots, gone, right)

    blank = jnp.zeros((channels, channels), bf16)
    for kernel_ref, w_ref in ((near_ref, wn_ref), (far_ref, wf_ref)):
        for a in range(4):
            for b in range(3):
                at = (a * 3 + b) * channels
                w_ref[at : at + channels, :channels] = kernel_ref[a, b] if a < 3 else blank
                w_ref[at : at + channels, channels:] = kernel_ref[a - 1, b] if a > 0 else blank

    span = cols + 8
    shifted = [col_buf[2 + 2 * b : 2 + 2 * b + span, :] for b in range(3)]
    taps = jnp.concatenate(shifted, axis=1)

    def fill(r):
        row = row_buf[pl.ds(r + 2, 1), :]
        triple = jnp.concatenate([row, row, row], axis=1)
        xn_ref[r] = jnp.maximum(triple + taps, 0.0).astype(bf16)

    def near_step(g):
        start = g * 8
        lhs = []
        for k in (0, 1, 4, 5):
            lhs.append(jnp.concatenate([xn_ref[start + k + 2 * a] for a in range(4)], axis=1))
        got = jnp.dot(jnp.concatenate(lhs, axis=0), wn_ref[...], preferred_element_type=f32)
        for n, k in enumerate((0, 1, 4, 5)):
            for side in range(2):
                r = start + k + 2 * side
                part = got[n * span : (n + 1) * span, side * channels : (side + 1) * channels]
                first = part + row_buf[pl.ds(r + 4, 1), :] + shifted[1]
                centre = first[4 : 4 + cols]
                first_ref[r] = centre
                hidden = jnp.concatenate([first[:cols], centre, first[8 : 8 + cols]], axis=1)
                xf_ref[r] = jnp.maximum(hidden, 0.0).astype(bf16)

    def far_step(g):
        start = g * 8
        lhs = []
        for k in range(4):
            lhs.append(jnp.concatenate([xf_ref[start + k + 4 * a] for a in range(4)], axis=1))
        got = jnp.dot(jnp.concatenate(lhs, axis=0), wf_ref[...], preferred_element_type=f32)
        for side in range(2):
            for k in range(4):
                part = got[k * cols : (k + 1) * cols, side * channels : (side + 1) * channels]
                second_ref[4 * side + k] = part + first_ref[start + 4 * side + k + 4]

    def transition_step(g):
        start = g * 8
        second = second_ref[...].reshape(8 * cols, channels)
        centred = second - jnp.mean(second, axis=-1, keepdims=True)
        variance = jnp.mean(centred * centred, axis=-1, keepdims=True)
        layer = (centred * lax.rsqrt(variance + LAYER_EPSILON) * gain_ref[...].astype(f32)).astype(bf16)
        middle = jnp.dot(layer, in_ref[...], preferred_element_type=f32)
        middle = jnp.maximum(middle, 0.0).astype(bf16)
        result = (second + jnp.dot(middle, tout_ref[...], preferred_element_type=f32)).astype(bf16)
        for k in range(8):
            out_ref[start + k] = result[k * cols : (k + 1) * cols]

    last = rows // 8
    for r in range(12):
        fill(r)

    def fill_for(g):
        for r in range(8):
            fill(g * 8 + 4 + r)

    near_step(0)
    fill_for(1)
    near_step(1)
    fill_for(2)
    far_step(0)
    near_step(2)
    fill_for(3)

    def steady(g, carry):
        near_step(g)
        transition_step(g - 3)
        far_step(g - 2)

        @pl.when(g < last)
        def _():
            fill_for(g + 1)

        return carry

    lax.fori_loop(3, last + 1, steady, 0)
    transition_step(last - 2)
    far_step(last - 1)
    transition_step(last - 1)


def pair_map(place, row, got, near, far, gain, trans_in, trans_out, order):
    rows, channels = row.shape
    cols = 2 * rows
    vmem = pl.BlockSpec(memory_space=pltpu.VMEM)
    return pl.pallas_call(
        pair_kernel,
        in_specs=[pl.BlockSpec(memory_space=pltpu.SMEM)] + [vmem] * 7 + [pl.BlockSpec(memory_space=pl.ANY)],
        out_specs=vmem,
        out_shape=jax.ShapeDtypeStruct((rows, cols, channels), bf16),
        scratch_shapes=[
            pltpu.VMEM((rows + 16, channels), f32),
            pltpu.VMEM((cols + 16, channels), f32),
            pltpu.VMEM((12 * channels, 2 * channels), bf16),
            pltpu.VMEM((12 * channels, 2 * channels), bf16),
            pltpu.VMEM((rows + 12, cols + 8, 3 * channels), bf16),
            pltpu.VMEM((rows + 8, cols, 3 * channels), bf16),
            pltpu.VMEM((rows + 8, cols, channels), f32),
            pltpu.VMEM((8, cols, channels), f32),
        ],
        compiler_params=params(),
        name="pair_map",
        cost_estimate=pl.CostEstimate(flops=14_000_000_000, bytes_accessed=3_000_000, transcendentals=0),
    )(place, row, got, near, far, gain, trans_in, trans_out, order)


def prepare_kernel(place_ref, seq_hbm, w_hbm, low_ref, high_ref, seq_out_ref, seq_buf, w_buf, sems):
    col = place_ref[1]
    other = lax.rem(col + 4, 8)
    windows = [pl.ds(pl.multiple_of((c * 3 // 2) * 128, 128), 256) for c in (col, other)]
    copies = []
    for h in range(4):
        row = pl.multiple_of((col // 4 * 4 + h) * HEAD, HEAD)
        for k, window in enumerate(windows):
            target = w_buf.at[pl.ds(h * 256, HEAD), pl.ds(256 * k, 256)]
            copies.append(pltpu.make_async_copy(w_hbm.at[pl.ds(row, HEAD), window], target, sems.at[2 * h + k]))
    copies.append(pltpu.make_async_copy(seq_hbm.at[:, windows[0]], seq_buf, sems.at[8]))
    for copy in copies:
        copy.start()
    for h in range(4):
        w_buf[h * 256 + HEAD : (h + 1) * 256, :] = jnp.zeros((64, 512), bf16)
    for copy in copies:
        copy.wait()
    for h in range(4):
        turned = w_buf[h * 256 : (h + 1) * 256, :].astype(f32).T
        low_ref[:, h * 256 : (h + 1) * 256] = turned.astype(bf16)
        high_ref[:, h * 256 : (h + 1) * 256] = pltpu.roll(turned, 64, axis=1).astype(bf16)
    seq_out_ref[...] = seq_buf[...].astype(f32).T.astype(bf16)


def prepare_trunk(place, sequence, out_weight):
    vmem = pl.BlockSpec(memory_space=pltpu.VMEM)
    hbm = pl.BlockSpec(memory_space=pl.ANY)
    rows = sequence.shape[0]
    return pl.pallas_call(
        prepare_kernel,
        in_specs=[pl.BlockSpec(memory_space=pltpu.SMEM)] + [hbm] * 2,
        out_specs=[vmem] * 3,
        out_shape=[jax.ShapeDtypeStruct((512, 1024), bf16)] * 2 + [jax.ShapeDtypeStruct((256, rows), bf16)],
        scratch_shapes=[
            pltpu.VMEM((rows, 256), bf16),
            pltpu.VMEM((4 * 256, 512), bf16),
            pltpu.SemaphoreType.DMA((9,)),
        ],
        compiler_params=params(),
        name="prepare_trunk",
    )(place, sequence, out_weight)


def trunk_kernel(place_ref, near_hbm, low_hbm, high_hbm, seq_hbm, mine_ref, sent_ref, all_buf, low, high, seq, turned, sems):
    n = all_buf.shape[1]
    copies = []
    for m, (source, target) in enumerate(((low_hbm, low), (high_hbm, high), (seq_hbm, seq))):
        copies.append(pltpu.make_async_copy(source, target, sems.at[m]))
    for h in range(4):
        copies.append(pltpu.make_async_copy(near_hbm.at[pl.ds(h * n, n)], all_buf.at[h], sems.at[3 + h]))
    order = (0, 3, 4, 5, 6, 1, 2)
    for m in order:
        copies[m].start()
    for m in order[:5]:
        copies[m].wait()
    for side, weight in ((0, low), (1, high)):
        if side == 1:
            copies[1].wait()
        rhs = jnp.concatenate([all_buf[h][:, 128 * side : 128 * side + 256] for h in range(4)], axis=1)
        turned[:, side * n : (side + 1) * n] = turned_dot(weight[...], rhs)
    copies[2].wait()
    offset = lax.rem(place_ref[1], 2) * 64
    mine = pl.ds(pl.multiple_of(offset, 64), HEAD)
    mine_ref[...] = turned[mine, :] + seq[mine, :].astype(f32)
    sent_ref[...] = turned[pl.ds(pl.multiple_of(256 + offset, 64), HEAD), :].astype(bf16)


def trunk_parts(place, near, low, high, seq):
    vmem = pl.BlockSpec(memory_space=pltpu.VMEM)
    hbm = pl.BlockSpec(memory_space=pl.ANY)
    rows = seq.shape[1]
    return pl.pallas_call(
        trunk_kernel,
        in_specs=[pl.BlockSpec(memory_space=pltpu.SMEM)] + [hbm] * 4,
        out_specs=[vmem] * 2,
        out_shape=[jax.ShapeDtypeStruct((HEAD, rows), f32), jax.ShapeDtypeStruct((HEAD, rows), bf16)],
        scratch_shapes=[
            pltpu.VMEM((4, rows // 2, 2 * HEAD), bf16),
            pltpu.VMEM(low.shape, bf16),
            pltpu.VMEM(high.shape, bf16),
            pltpu.VMEM(seq.shape, bf16),
            pltpu.VMEM((512, rows), f32),
            pltpu.SemaphoreType.DMA((7,)),
        ],
        compiler_params=params(),
        name="trunk_parts",
        cost_estimate=pl.CostEstimate(flops=1_100_000_000, bytes_accessed=5_000_000, transcendentals=0),
    )(place, near, low, high, seq)


def per_device(
    sequence,
    norm_gain,
    query_weight,
    key_weight,
    value_weight,
    out_weight,
    pool_gain,
    row_weight,
    column_weight,
    conv_near,
    conv_far,
    trans_gain,
    trans_in,
    trans_out,
):
    place = jnp.stack([lax.axis_index("ctx"), lax.axis_index("col")]).astype(jnp.int32)
    spots = range(16)
    cols = range(8)
    to_core = [(i, i ^ 1) for i in spots]
    to_z = [(i, i ^ 8) for i in spots]
    to_up = [(i, (i & 8) | ((i + 2) & 7)) for i in spots]
    to_down = [(i, (i & 8) | ((i - 2) & 7)) for i in spots]

    def send(x, perm):
        return lax.ppermute(x, "ctx", perm)

    kv = project_kv(sequence, norm_gain, key_weight, value_weight)
    kv_core = send(kv, to_core)
    kv_below = send(kv, to_up)
    kv_above = send(kv, to_down)
    query, mean_low, mean_high = project_q(sequence, norm_gain, query_weight)
    query_z = send(query, to_z)
    state = attend(query, [kv, kv_core])
    gain_row = pool_gain.reshape(1, -1)
    trans_row = trans_gain.reshape(1, -1)
    weights_low, weights_high, seq_cols = prepare_trunk(place, sequence, out_weight)
    low, high = cut(kv_below, kv_above, state, seq_cols)
    far_below = send(low, to_up)
    far_above = send(high, to_down)
    twin = [send(kv_below, to_core), send(kv_above, to_core)]
    state_z = attend(query_z, [kv, kv_core, kv_below, kv_above], orders=(low, gain_row, trans_row, place))
    opposite = join(far_below, far_above, state_z)
    opposite_core = send(opposite, to_core)
    state_z = attend(query_z, twin, state_z)
    returned = attend(query_z, [opposite, opposite_core], state_z, mode="remote")
    other = send(returned, to_z)
    rest = [kv_below, kv_above, *twin, opposite, opposite_core]
    mine, log = attend(query, rest, state, mode="final")
    attended, pool = merge(mine, log, other)

    along_y = [[0, 1, 2, 3], [4, 5, 6, 7]]
    near_heads = lax.all_gather(attended, "col", axis=0, tiled=True, axis_index_groups=along_y)
    pools = lax.all_to_all(pool, "col", 0, 0)
    row, sent = features(
        pools, mean_low, mean_high, out_weight, gain_row, row_weight, column_weight, lax.axis_size("ctx")
    )
    got = lax.all_to_all(sent, "ctx", 0, 0)
    mine_cols, sent_cols = trunk_parts(place, near_heads, weights_low, weights_high, seq_cols)
    got_cols = lax.ppermute(sent_cols, "col", [(i, i ^ 4) for i in cols])
    pair_out = pair_map(
        place, row, got, conv_near, conv_far, trans_row, trans_in, trans_out, sent_cols
    )
    trunk_out = (mine_cols + got_cols.astype(f32)).astype(bf16).T
    return (trunk_out, pair_out)


def solution(mesh):
    return jax.shard_map(
        per_device,
        mesh=mesh,
        in_specs=(
            P("ctx", None),
            P(),
            P(None, "col"),
            P(None, "col"),
            P(None, "col"),
            P(),
            P(),
            P(),
            P(),
            P(),
            P(),
            P(),
            P(),
            P(),
        ),
        out_specs=(P("ctx", "col"), P("ctx", "col", None)),
        check_vma=False,
    )
```

```python
import functools
import math

import jax
import jax.numpy as jnp
from jax import lax
from jax.experimental import pallas as pl
from jax.experimental.pallas import tpu as pltpu
from jax.sharding import PartitionSpec as P

POOL = 16
HEAD = 192
EPSILON = 1e-06
LAYER_EPSILON = 1e-05
OUTSIDE = -1e30
SCALE = math.log2(math.e) / math.sqrt(HEAD)
bf16 = jnp.bfloat16
f32 = jnp.float32
VMEM = 56 * 2**20


def params(limit=VMEM):
    return pltpu.CompilerParams(vmem_limit_bytes=limit)


def lanes_of(shape):
    return lax.broadcasted_iota(jnp.int32, shape, len(shape) - 1)


def pack_lanes(low, high):
    rolled = pltpu.roll(high, 64, axis=1)
    middle = jnp.where(lanes_of(rolled.shape) < 64, pltpu.roll(low, 128, axis=1), rolled)
    return jnp.concatenate([low[:, :128], middle], axis=1)


def unpack_query(packed):
    wide = pltpu.roll(packed[:, :256].astype(f32), 64, axis=1)
    lane = lanes_of(wide.shape)
    low = jnp.where(lane < 64, 0.0, wide).astype(bf16)
    high = jnp.where(lane < 64, 0.0, packed[:, 128:].astype(f32)).astype(bf16)
    return jnp.concatenate([low, high], axis=0)


def normalised(x, gain):
    square = jnp.mean(x * x, axis=-1, keepdims=True)
    return (x * lax.rsqrt(square + EPSILON) * gain).astype(bf16)


def turned_dot(a, b):
    return lax.dot_general(a, b, (((1,), (1,)), ((), ())), preferred_element_type=f32)


def project_kv_kernel(seq_ref, gain_ref, wk_ref, wv_ref, kv_ref):
    gain = gain_ref[...].astype(f32).reshape(1, -1)
    weights = jnp.concatenate([wv_ref[...], wk_ref[...]], axis=0)
    rows = seq_ref.shape[0]
    part = rows // 2
    for start in range(0, rows, part):
        normed = normalised(seq_ref[start : start + part, :].astype(f32), gain)
        kv_ref[start : start + part, :] = turned_dot(normed, weights).astype(bf16)


def project_kv(sequence, gain, wk, wv):
    rows, feat = sequence.shape
    steps = 2
    whole = lambda a: pl.BlockSpec(a.shape, lambda t: (0,) * a.ndim)
    wk, wv = wk.T, wv.T
    return pl.pallas_call(
        project_kv_kernel,
        grid=(steps,),
        in_specs=[pl.BlockSpec((rows // steps, feat), lambda t: (t, 0)), whole(gain), whole(wk), whole(wv)],
        out_specs=pl.BlockSpec((rows // steps, 2 * HEAD), lambda t: (t, 0)),
        out_shape=jax.ShapeDtypeStruct((rows, 2 * HEAD), bf16),
        compiler_params=params(),
        name="project_kv",
        cost_estimate=pl.CostEstimate(flops=4 * rows * feat * HEAD, bytes_accessed=5_000_000, transcendentals=0),
    )(sequence, gain, wk, wv)


def project_q_kernel(low_ref, high_ref, gain_ref, wq_ref, q_ref, ml_ref, mh_ref):
    gain = gain_ref[...].astype(f32).reshape(1, -1)
    rows = low_ref.shape[0]
    part = rows // 2
    for start in range(0, rows, part):
        halves = []
        for ref, mean_ref in ((low_ref, ml_ref), (high_ref, mh_ref)):
            x = ref[start : start + part, :].astype(f32)
            mean = jnp.mean(x.reshape(part // POOL, POOL, x.shape[1]), axis=1)
            mean_ref[start // POOL : (start + part) // POOL, :] = mean
            halves.append(normalised(x, gain))
        q = turned_dot(jnp.concatenate(halves, axis=0), wq_ref[...]) * SCALE
        q = jnp.concatenate([q, jnp.zeros((2 * part, 64), f32)], axis=1)
        q_ref[start : start + part, :] = pack_lanes(q[:part], q[part:]).astype(bf16)


def project_q(sequence, gain, wq):
    rows, feat = sequence.shape
    steps = 2
    tile = rows // 2 // steps
    whole = lambda a: pl.BlockSpec(a.shape, lambda t: (0,) * a.ndim)
    wq = wq.T
    return pl.pallas_call(
        project_q_kernel,
        grid=(steps,),
        in_specs=[
            pl.BlockSpec((tile, feat), lambda t: (t, 0)),
            pl.BlockSpec((tile, feat), lambda t: (t + steps, 0)),
            whole(gain),
            whole(wq),
        ],
        out_specs=[
            pl.BlockSpec((tile, 2 * HEAD), lambda t: (t, 0)),
            pl.BlockSpec((tile // POOL, feat), lambda t: (t, 0)),
            pl.BlockSpec((tile // POOL, feat), lambda t: (t, 0)),
        ],
        out_shape=[
            jax.ShapeDtypeStruct((rows // 2, 2 * HEAD), bf16),
            jax.ShapeDtypeStruct((rows // 2 // POOL, feat), f32),
            jax.ShapeDtypeStruct((rows // 2 // POOL, feat), f32),
        ],
        compiler_params=params(),
        name="project_q",
        cost_estimate=pl.CostEstimate(flops=2 * rows * feat * HEAD, bytes_accessed=5_000_000, transcendentals=0),
    )(sequence, sequence, gain, wq)


SUB = 256


def log_rows(logs):
    rows = []
    for log in logs:
        for g in range(log.shape[0] // 128):
            block = jnp.broadcast_to(log[g * 128 : (g + 1) * 128], (128, 128))
            rows.append(block.T[:1])
    return jnp.concatenate(rows, axis=0)


def attend_kernel(*refs, count, carried, mode, orders):
    q_ref = refs[0]
    kv_refs = refs[1 : 1 + count]
    rest = list(refs[1 + count :])
    state_ref = rest.pop(0) if carried else None
    rest = rest[orders:]
    out_ref = rest.pop(0)
    log_ref = rest.pop(0) if mode == "final" else None
    v_buf = rest[0]
    queries = unpack_query(q_ref[...])
    subs = queries.shape[0] // SUB
    half = subs // 2
    order = range(subs) if mode == "state" else [i + s * half for i in range(half) for s in range(2)]
    units = [(i, c) for i in order for c in range(count)]
    size = kv_refs[0].shape[0]

    def score(unit):
        i, c = unit
        if i == 0:
            v = kv_refs[c][:, :256]
            lane = lanes_of(v.shape)
            v_buf[c * size : (c + 1) * size, :] = jnp.where(
                lane < HEAD, v, jnp.where(lane == HEAD, 1.0, 0.0).astype(bf16)
            )
        return turned_dot(queries[i * SUB : (i + 1) * SUB], kv_refs[c][:, 128:])

    following = score(units[0])
    results = {}
    top = total = None
    for n, (i, c) in enumerate(units):
        scores = following
        if n + 1 < len(units):
            following = score(units[n + 1])
        here = jnp.max(scores, axis=1, keepdims=True)
        new = here if c == 0 else jnp.maximum(top, here)
        weights = jnp.exp2(scores - new).astype(bf16)
        mixed = jnp.dot(weights, v_buf[c * size : (c + 1) * size, :], preferred_element_type=f32)
        total = mixed if c == 0 else total * jnp.exp2(top - new) + mixed
        top = new
        if c < count - 1:
            continue
        if carried:
            before = state_ref[i * SUB : (i + 1) * SUB, :]
            old = before[:, HEAD + 1 : HEAD + 2]
            new = jnp.maximum(top, old)
            total = total * jnp.exp2(top - new) + before * jnp.exp2(old - new)
            top = new
        if mode == "state":
            out_ref[i * SUB : (i + 1) * SUB, :] = jnp.where(lanes_of(total.shape) == HEAD + 1, top, total)
            continue
        sums = total[:, HEAD : HEAD + 1]
        results[i] = (total * (1.0 / sums), top + jnp.log2(sums))
        if i >= half:
            packed = pack_lanes(results[i - half][0], results[i][0])
            out_ref[(i - half) * SUB : (i - half + 1) * SUB, :] = packed.astype(out_ref.dtype)
    if mode != "state":
        rows = log_rows([results[i][1] for i in range(subs)])
    if mode == "remote":
        rows = jnp.concatenate([rows, jnp.zeros((16 - rows.shape[0], 128), f32)], axis=0)
        first = rows.astype(bf16)
        left = rows - first.astype(f32)
        second = left.astype(bf16)
        third = (left - second.astype(f32)).astype(bf16)
        out_ref[half * SUB :, :] = jnp.concatenate([first, second, third], axis=1)
    if mode == "final":
        log_ref[...] = rows


def attend(query, kvs, state=None, mode="state", orders=()):
    rows = query.shape[0]
    keys = sum(kv.shape[0] for kv in kvs)
    args = [query, *kvs] + ([] if state is None else [state])
    out_shape = {
        "state": [jax.ShapeDtypeStruct((2 * rows, 256), f32)],
        "remote": [jax.ShapeDtypeStruct((rows + 16, 2 * HEAD), bf16)],
        "final": [
            jax.ShapeDtypeStruct((rows, 2 * HEAD), f32),
            jax.ShapeDtypeStruct((2 * rows // 128, 128), f32),
        ],
    }[mode]
    vmem = pl.BlockSpec(memory_space=pltpu.VMEM)
    out = pl.pallas_call(
        functools.partial(
            attend_kernel, count=len(kvs), carried=state is not None, mode=mode, orders=len(orders)
        ),
        in_specs=[vmem] * len(args) + [pl.BlockSpec(memory_space=pl.ANY)] * len(orders),
        out_specs=[vmem] * len(out_shape),
        out_shape=out_shape,
        scratch_shapes=[pltpu.VMEM((keys, 256), bf16)],
        compiler_params=params(36 * 2**20),
        name="attend_" + mode,
        cost_estimate=pl.CostEstimate(
            flops=2 * 2 * rows * keys * 512, bytes_accessed=4_000_000, transcendentals=2 * rows * keys
        ),
    )(*args, *orders)
    return out if mode == "final" else out[0]


def cut_kernel(below_ref, above_ref, *refs):
    out_low_ref, out_high_ref, sems = refs[-3:]
    n = out_low_ref.shape[0]
    low = pltpu.make_async_copy(below_ref.at[pl.ds(0, n)], out_low_ref, sems.at[0])
    high = pltpu.make_async_copy(above_ref.at[pl.ds(n, n)], out_high_ref, sems.at[1])
    low.start()
    high.start()
    low.wait()
    high.wait()


def cut(below, above, *orders):
    hbm = pl.BlockSpec(memory_space=pl.ANY)
    part = jax.ShapeDtypeStruct((below.shape[0] // 2, below.shape[1]), below.dtype)
    return pl.pallas_call(
        cut_kernel,
        in_specs=[hbm] * (2 + len(orders)),
        out_specs=[hbm] * 2,
        out_shape=[part] * 2,
        scratch_shapes=[pltpu.SemaphoreType.DMA((2,))],
        compiler_params=params(2**20),
        name="cut",
    )(below, above, *orders)


def join_kernel(low_ref, high_ref, order_ref, out_ref, sems):
    n = low_ref.shape[0]
    low = pltpu.make_async_copy(low_ref, out_ref.at[pl.ds(0, n)], sems.at[0])
    high = pltpu.make_async_copy(high_ref, out_ref.at[pl.ds(n, n)], sems.at[1])
    low.start()
    high.start()
    low.wait()
    high.wait()


def join(low, high, order):
    hbm = pl.BlockSpec(memory_space=pl.ANY)
    return pl.pallas_call(
        join_kernel,
        in_specs=[hbm] * 3,
        out_specs=hbm,
        out_shape=jax.ShapeDtypeStruct((2 * low.shape[0], low.shape[1]), low.dtype),
        scratch_shapes=[pltpu.SemaphoreType.DMA((2,))],
        compiler_params=params(2**20),
        name="join",
    )(low, high, order)


def relay_kernel(x_ref, *refs):
    out_ref, sem = refs[-2:]
    copy = pltpu.make_async_copy(x_ref, out_ref, sem)
    copy.start()
    copy.wait()


def relay(x, *orders):
    hbm = pl.BlockSpec(memory_space=pl.ANY)
    return pl.pallas_call(
        relay_kernel,
        in_specs=[hbm] * (1 + len(orders)),
        out_specs=hbm,
        out_shape=jax.ShapeDtypeStruct(x.shape, x.dtype),
        scratch_shapes=[pltpu.SemaphoreType.DMA],
        compiler_params=params(2**20),
        name="relay",
    )(x, *orders)


def merge_kernel(mine_ref, log_ref, other_ref, out_ref, pool_ref):
    n = out_ref.shape[0]
    stats = other_ref[n:, :].astype(f32)
    rows = (stats[:, :128] + stats[:, 128:256] + stats[:, 256:])[: 2 * n // 128]
    share = 1.0 / (1.0 + jnp.exp2(log_ref[...] - rows))
    columns = []
    for g in range(2 * n // 128):
        columns.append(jnp.broadcast_to(share[g : g + 1], (128, 128)).T)
    low = jnp.concatenate(columns[: n // 128], axis=0)
    high = jnp.concatenate(columns[n // 128 :], axis=0)
    middle = jnp.where(lanes_of(low.shape) < 64, low, high)
    share = jnp.concatenate([low, middle, high], axis=1)
    mine = mine_ref[...]
    attended = (mine + share * (other_ref[:n, :].astype(f32) - mine)).astype(bf16)
    out_ref[...] = attended
    wide = attended.astype(f32)
    pool = jnp.mean(wide.reshape(n // POOL, POOL, wide.shape[1]), axis=1).astype(bf16)
    for k in range(pool_ref.shape[0]):
        pool_ref[k] = pool


def merge(mine, log, other):
    rows = mine.shape[0]
    vmem = pl.BlockSpec(memory_space=pltpu.VMEM)
    return pl.pallas_call(
        merge_kernel,
        in_specs=[vmem] * 3,
        out_specs=[vmem] * 2,
        out_shape=[
            jax.ShapeDtypeStruct((rows, 2 * HEAD), bf16),
            jax.ShapeDtypeStruct((8, rows // POOL, 2 * HEAD), bf16),
        ],
        compiler_params=params(16 * 2**20),
        name="merge",
    )(mine, log, other)


def features_kernel(*refs):
    sources, rest = refs[:7], refs[7:]
    rout_ref, sent_ref, pool_ref, ml_ref, mh_ref, w_ref, gain_ref, row_ref, col_ref, sems = rest
    held = (pool_ref, ml_ref, mh_ref, w_ref, gain_ref, row_ref, col_ref)
    parts = 6
    depth = w_ref.shape[0] // parts
    copies = {}
    for n in (0, 3, 1, 2, 4, 5, 6):
        if n == 3:
            w_copies = []
            for p in range(parts):
                piece = pl.ds(p * depth, depth)
                w_copies.append(pltpu.make_async_copy(sources[3].at[piece], w_ref.at[piece], sems.at[p]))
                w_copies[p].start()
        else:
            copies[n] = pltpu.make_async_copy(sources[n], held[n], sems.at[parts + n])
            copies[n].start()
    copies[0].wait()
    heads = []
    for h in range(8):
        packed = pool_ref[h].astype(f32)
        low, high = packed[:, :256], pltpu.roll(packed[:, 128:], 192, axis=1)
        heads.append(jnp.concatenate([low, high], axis=0)[:, :HEAD])
    lhs = jnp.concatenate(heads, axis=1).astype(bf16)
    pooled = None
    for p in range(parts):
        w_copies[p].wait()
        piece = slice(p * depth, (p + 1) * depth)
        product = jnp.dot(lhs[:, piece], w_ref[piece, :], preferred_element_type=f32)
        pooled = product if pooled is None else pooled + product
    for n in (1, 2, 4, 5, 6):
        copies[n].wait()
    pooled = pooled + jnp.concatenate([ml_ref[...], mh_ref[...]], axis=0)
    inverse = lax.rsqrt(jnp.mean(pooled * pooled, axis=-1, keepdims=True) + EPSILON)
    scaled = (pooled * gain_ref[...].astype(f32)).astype(bf16)
    weights = jnp.concatenate([row_ref[...], col_ref[...]], axis=1)
    got = (inverse * jnp.dot(scaled, weights, preferred_element_type=f32)).astype(bf16).astype(f32)
    channels = rout_ref.shape[1]
    row, col = got[:, :channels], got[:, channels:]
    rout_ref[...] = row.astype(bf16)
    sent = jnp.concatenate([col, row[:8], row[-8:]], axis=0).astype(bf16)
    for k in range(sent_ref.shape[0]):
        sent_ref[k] = sent


def features(pools, mean_low, mean_high, out_weight, gain, row_weight, column_weight, copies):
    rows = 2 * mean_low.shape[0]
    channels = row_weight.shape[1]
    vmem = pl.BlockSpec(memory_space=pltpu.VMEM)
    hbm = pl.BlockSpec(memory_space=pl.ANY)
    return pl.pallas_call(
        features_kernel,
        in_specs=[hbm] * 7,
        out_specs=[vmem] * 2,
        out_shape=[
            jax.ShapeDtypeStruct((rows, channels), bf16),
            jax.ShapeDtypeStruct((copies, rows + 16, channels), bf16),
        ],
        scratch_shapes=[
            pltpu.VMEM(a.shape, a.dtype)
            for a in (pools, mean_low, mean_high, out_weight, gain, row_weight, column_weight)
        ]
        + [pltpu.SemaphoreType.DMA((13,))],
        compiler_params=params(),
        name="features",
    )(pools, mean_low, mean_high, out_weight, gain, row_weight, column_weight)


def pair_kernel(
    place_ref, row_ref, got_ref, near_ref, far_ref, gain_ref, in_ref, tout_ref, order_ref,
    out_ref, row_buf, col_buf, wn_ref, wf_ref, xn_ref, xf_ref, first_ref, second_ref,
):
    rows, cols, channels = out_ref.shape
    ctx, col = place_ref[0], place_ref[1]
    gone = jnp.full((8, channels), OUTSIDE, f32)
    spots = got_ref.shape[0]
    above = got_ref[jnp.maximum(ctx - 1, 0)][rows + 8 :].astype(f32)
    below = got_ref[jnp.minimum(ctx + 1, spots - 1)][rows : rows + 8].astype(f32)
    row_buf[:8] = jnp.where(ctx == 0, gone, above)
    row_buf[8 : 8 + rows] = row_ref[...].astype(f32)
    row_buf[8 + rows :] = jnp.where(ctx == spots - 1, gone, below)
    half = cols // 2
    left = got_ref[jnp.maximum(2 * col - 1, 0)][half - 8 : half].astype(f32)
    right = got_ref[jnp.minimum(2 * col + 2, spots - 1)][:8].astype(f32)
    col_buf[:8] = jnp.where(col == 0, gone, left)
    col_buf[8 : 8 + half] = got_ref[2 * col][:half].astype(f32)
    col_buf[8 + half : 8 + cols] = got_ref[2 * col + 1][:half].astype(f32)
    col_buf[8 + cols :] = jnp.where(2 * col + 2 >= spots, gone, right)

    blank = jnp.zeros((channels, channels), bf16)
    for kernel_ref, w_ref in ((near_ref, wn_ref), (far_ref, wf_ref)):
        for a in range(4):
            for b in range(3):
                at = (a * 3 + b) * channels
                w_ref[at : at + channels, :channels] = kernel_ref[a, b] if a < 3 else blank
                w_ref[at : at + channels, channels:] = kernel_ref[a - 1, b] if a > 0 else blank

    span = cols + 8
    shifted = [col_buf[2 + 2 * b : 2 + 2 * b + span, :] for b in range(3)]
    taps = jnp.concatenate(shifted, axis=1)

    def fill(r):
        row = row_buf[pl.ds(r + 2, 1), :]
        triple = jnp.concatenate([row, row, row], axis=1)
        xn_ref[r] = jnp.maximum(triple + taps, 0.0).astype(bf16)

    def near_step(g):
        start = g * 8
        lhs = []
        for k in (0, 1, 4, 5):
            lhs.append(jnp.concatenate([xn_ref[start + k + 2 * a] for a in range(4)], axis=1))
        got = jnp.dot(jnp.concatenate(lhs, axis=0), wn_ref[...], preferred_element_type=f32)
        for n, k in enumerate((0, 1, 4, 5)):
            for side in range(2):
                r = start + k + 2 * side
                part = got[n * span : (n + 1) * span, side * channels : (side + 1) * channels]
                first = part + row_buf[pl.ds(r + 4, 1), :] + shifted[1]
                centre = first[4 : 4 + cols]
                first_ref[r] = centre
                hidden = jnp.concatenate([first[:cols], centre, first[8 : 8 + cols]], axis=1)
                xf_ref[r] = jnp.maximum(hidden, 0.0).astype(bf16)

    def far_step(g):
        start = g * 8
        lhs = []
        for k in range(4):
            lhs.append(jnp.concatenate([xf_ref[start + k + 4 * a] for a in range(4)], axis=1))
        got = jnp.dot(jnp.concatenate(lhs, axis=0), wf_ref[...], preferred_element_type=f32)
        for side in range(2):
            for k in range(4):
                part = got[k * cols : (k + 1) * cols, side * channels : (side + 1) * channels]
                second_ref[4 * side + k] = part + first_ref[start + 4 * side + k + 4]

    def transition_step(g):
        start = g * 8
        second = second_ref[...].reshape(8 * cols, channels)
        centred = second - jnp.mean(second, axis=-1, keepdims=True)
        variance = jnp.mean(centred * centred, axis=-1, keepdims=True)
        layer = (centred * lax.rsqrt(variance + LAYER_EPSILON) * gain_ref[...].astype(f32)).astype(bf16)
        middle = jnp.dot(layer, in_ref[...], preferred_element_type=f32)
        middle = jnp.maximum(middle, 0.0).astype(bf16)
        result = (second + jnp.dot(middle, tout_ref[...], preferred_element_type=f32)).astype(bf16)
        for k in range(8):
            out_ref[start + k] = result[k * cols : (k + 1) * cols]

    last = rows // 8
    for r in range(12):
        fill(r)

    def fill_for(g):
        for r in range(8):
            fill(g * 8 + 4 + r)

    near_step(0)
    fill_for(1)
    near_step(1)
    fill_for(2)
    far_step(0)
    near_step(2)
    fill_for(3)

    def steady(g, carry):
        near_step(g)
        transition_step(g - 3)
        far_step(g - 2)

        @pl.when(g < last)
        def _():
            fill_for(g + 1)

        return carry

    lax.fori_loop(3, last + 1, steady, 0)
    transition_step(last - 2)
    far_step(last - 1)
    transition_step(last - 1)


def pair_map(place, row, got, near, far, gain, trans_in, trans_out, order):
    rows, channels = row.shape
    cols = 2 * rows
    vmem = pl.BlockSpec(memory_space=pltpu.VMEM)
    return pl.pallas_call(
        pair_kernel,
        in_specs=[pl.BlockSpec(memory_space=pltpu.SMEM)] + [vmem] * 7 + [pl.BlockSpec(memory_space=pl.ANY)],
        out_specs=vmem,
        out_shape=jax.ShapeDtypeStruct((rows, cols, channels), bf16),
        scratch_shapes=[
            pltpu.VMEM((rows + 16, channels), f32),
            pltpu.VMEM((cols + 16, channels), f32),
            pltpu.VMEM((12 * channels, 2 * channels), bf16),
            pltpu.VMEM((12 * channels, 2 * channels), bf16),
            pltpu.VMEM((rows + 12, cols + 8, 3 * channels), bf16),
            pltpu.VMEM((rows + 8, cols, 3 * channels), bf16),
            pltpu.VMEM((rows + 8, cols, channels), f32),
            pltpu.VMEM((8, cols, channels), f32),
        ],
        compiler_params=params(),
        name="pair_map",
        cost_estimate=pl.CostEstimate(flops=14_000_000_000, bytes_accessed=3_000_000, transcendentals=0),
    )(place, row, got, near, far, gain, trans_in, trans_out, order)


def prepare_kernel(place_ref, seq_hbm, w_hbm, low_ref, high_ref, seq_out_ref, seq_buf, w_buf, sems):
    col = place_ref[1]
    other = lax.rem(col + 4, 8)
    windows = [pl.ds(pl.multiple_of((c * 3 // 2) * 128, 128), 256) for c in (col, other)]
    copies = []
    for h in range(4):
        row = pl.multiple_of((col // 4 * 4 + h) * HEAD, HEAD)
        for k, window in enumerate(windows):
            target = w_buf.at[pl.ds(h * 256, HEAD), pl.ds(256 * k, 256)]
            copies.append(pltpu.make_async_copy(w_hbm.at[pl.ds(row, HEAD), window], target, sems.at[2 * h + k]))
    copies.append(pltpu.make_async_copy(seq_hbm.at[:, windows[0]], seq_buf, sems.at[8]))
    for copy in copies:
        copy.start()
    for h in range(4):
        w_buf[h * 256 + HEAD : (h + 1) * 256, :] = jnp.zeros((64, 512), bf16)
    for copy in copies:
        copy.wait()
    for h in range(4):
        turned = w_buf[h * 256 : (h + 1) * 256, :].astype(f32).T
        low_ref[:, h * 256 : (h + 1) * 256] = turned.astype(bf16)
        high_ref[:, h * 256 : (h + 1) * 256] = pltpu.roll(turned, 64, axis=1).astype(bf16)
    seq_out_ref[...] = seq_buf[...].astype(f32).T.astype(bf16)


def prepare_trunk(place, sequence, out_weight):
    vmem = pl.BlockSpec(memory_space=pltpu.VMEM)
    hbm = pl.BlockSpec(memory_space=pl.ANY)
    rows = sequence.shape[0]
    return pl.pallas_call(
        prepare_kernel,
        in_specs=[pl.BlockSpec(memory_space=pltpu.SMEM)] + [hbm] * 2,
        out_specs=[vmem] * 3,
        out_shape=[jax.ShapeDtypeStruct((512, 1024), bf16)] * 2 + [jax.ShapeDtypeStruct((256, rows), bf16)],
        scratch_shapes=[
            pltpu.VMEM((rows, 256), bf16),
            pltpu.VMEM((4 * 256, 512), bf16),
            pltpu.SemaphoreType.DMA((9,)),
        ],
        compiler_params=params(),
        name="prepare_trunk",
    )(place, sequence, out_weight)


def trunk_kernel(place_ref, near_hbm, low_hbm, high_hbm, seq_hbm, mine_ref, sent_ref, all_buf, low, high, seq, turned, sems):
    n = all_buf.shape[1]
    copies = []
    for m, (source, target) in enumerate(((low_hbm, low), (high_hbm, high), (seq_hbm, seq))):
        copies.append(pltpu.make_async_copy(source, target, sems.at[m]))
    for h in range(4):
        copies.append(pltpu.make_async_copy(near_hbm.at[pl.ds(h * n, n)], all_buf.at[h], sems.at[3 + h]))
    order = (0, 3, 4, 5, 6, 1, 2)
    for m in order:
        copies[m].start()
    for m in order[:5]:
        copies[m].wait()
    for side, weight in ((0, low), (1, high)):
        if side == 1:
            copies[1].wait()
        rhs = jnp.concatenate([all_buf[h][:, 128 * side : 128 * side + 256] for h in range(4)], axis=1)
        turned[:, side * n : (side + 1) * n] = turned_dot(weight[...], rhs)
    copies[2].wait()
    offset = lax.rem(place_ref[1], 2) * 64
    mine = pl.ds(pl.multiple_of(offset, 64), HEAD)
    mine_ref[...] = turned[mine, :] + seq[mine, :].astype(f32)
    sent_ref[...] = turned[pl.ds(pl.multiple_of(256 + offset, 64), HEAD), :].astype(bf16)


def trunk_parts(place, near, low, high, seq):
    vmem = pl.BlockSpec(memory_space=pltpu.VMEM)
    hbm = pl.BlockSpec(memory_space=pl.ANY)
    rows = seq.shape[1]
    return pl.pallas_call(
        trunk_kernel,
        in_specs=[pl.BlockSpec(memory_space=pltpu.SMEM)] + [hbm] * 4,
        out_specs=[vmem] * 2,
        out_shape=[jax.ShapeDtypeStruct((HEAD, rows), f32), jax.ShapeDtypeStruct((HEAD, rows), bf16)],
        scratch_shapes=[
            pltpu.VMEM((4, rows // 2, 2 * HEAD), bf16),
            pltpu.VMEM(low.shape, bf16),
            pltpu.VMEM(high.shape, bf16),
            pltpu.VMEM(seq.shape, bf16),
            pltpu.VMEM((512, rows), f32),
            pltpu.SemaphoreType.DMA((7,)),
        ],
        compiler_params=params(),
        name="trunk_parts",
        cost_estimate=pl.CostEstimate(flops=1_100_000_000, bytes_accessed=5_000_000, transcendentals=0),
    )(place, near, low, high, seq)


def per_device(
    sequence,
    norm_gain,
    query_weight,
    key_weight,
    value_weight,
    out_weight,
    pool_gain,
    row_weight,
    column_weight,
    conv_near,
    conv_far,
    trans_gain,
    trans_in,
    trans_out,
):
    place = jnp.stack([lax.axis_index("ctx"), lax.axis_index("col")]).astype(jnp.int32)
    spots = range(16)
    cols = range(8)
    to_core = [(i, i ^ 1) for i in spots]
    to_z = [(i, i ^ 8) for i in spots]
    to_up = [(i, (i & 8) | ((i + 2) & 7)) for i in spots]
    to_down = [(i, (i & 8) | ((i - 2) & 7)) for i in spots]

    def send(x, perm):
        return lax.ppermute(x, "ctx", perm)

    kv = project_kv(sequence, norm_gain, key_weight, value_weight)
    kv_core = send(kv, to_core)
    kv_below = send(kv, to_up)
    kv_above = send(kv, to_down)
    query, mean_low, mean_high = project_q(sequence, norm_gain, query_weight)
    query_z = send(query, to_z)
    state = attend(query, [kv])
    gain_row = pool_gain.reshape(1, -1)
    trans_row = trans_gain.reshape(1, -1)
    weights_low, weights_high, seq_cols = prepare_trunk(place, sequence, out_weight)
    low, high = cut(kv_below, kv_above, state, seq_cols)
    far_below = send(low, to_up)
    far_above = send(high, to_down)
    twin = [send(kv_below, to_core), send(kv_above, to_core)]
    state_z = attend(query_z, [kv, kv_core, kv_below, kv_above], orders=(low, gain_row, trans_row, place))
    opposite = join(far_below, far_above, state_z)
    opposite_core = send(opposite, to_core)
    state_z = attend(query_z, twin, state_z)
    returned = attend(query_z, [opposite, opposite_core], state_z, mode="remote")
    other = send(returned, to_z)
    rest = [kv_core, kv_below, kv_above, *twin, opposite, opposite_core]
    mine, log = attend(query, rest, state, mode="final")
    attended, pool = merge(mine, log, other)

    along_y = [[0, 1, 2, 3], [4, 5, 6, 7]]
    near_heads = lax.all_gather(attended, "col", axis=0, tiled=True, axis_index_groups=along_y)
    pools = lax.all_to_all(pool, "col", 0, 0)
    row, sent = features(
        pools, mean_low, mean_high, out_weight, gain_row, row_weight, column_weight, lax.axis_size("ctx")
    )
    got = lax.all_to_all(sent, "ctx", 0, 0)
    mine_cols, sent_cols = trunk_parts(place, near_heads, weights_low, weights_high, seq_cols)
    got_cols = lax.ppermute(sent_cols, "col", [(i, i ^ 4) for i in cols])
    pair_out = pair_map(
        place, row, got, conv_near, conv_far, trans_row, trans_in, trans_out, sent_cols
    )
    trunk_out = (mine_cols + got_cols.astype(f32)).astype(bf16).T
    return (trunk_out, pair_out)


def solution(mesh):
    return jax.shard_map(
        per_device,
        mesh=mesh,
        in_specs=(
            P("ctx", None),
            P(),
            P(None, "col"),
            P(None, "col"),
            P(None, "col"),
            P(),
            P(),
            P(),
            P(),
            P(),
            P(),
            P(),
            P(),
            P(),
        ),
        out_specs=(P("ctx", "col"), P("ctx", "col", None)),
        check_vma=False,
    )
```
